128 devices in a mesh: clus: 8 (over x, core), grp: 16 (over z, y).
Axes of the slice: x: 4, y: 4, z: 4, core: 2. Of those that a mesh axis runs over, the one named last changes fastest.
Arguments:
- embeddings: bfloat16 [262144, 1024], P(('clus', 'grp')), may hold values from -6 to 6
- labels: int32 [262144], P(('clus', 'grp')), may hold values from 0 to 3
- partner_block: int32 [128, 24], P(('clus', 'grp')), may hold values from 0 to 3
- own_block: int32 [128, 24], P(('clus', 'grp')), may hold values from 0 to 3
- live: int32 [128, 24], P(('clus', 'grp')), may hold values from 0 to 1, as said below
Outputs:
- best_similarity: float32 [262144], P(('clus', 'grp'))
The draws below stay inside these ranges and needn't reach their ends.
Inputs may be any that keep to these rules, and one draw needn't show every extreme that they name: live is 0 or 1; each device draws k from 1 to 4 and each of its slots is live with probability k / 4; one device of the whole mesh has every slot live.
All inputs are finite; a program needn't handle non-finite values.
Results may differ from the reference program's by a relative error of at most 0.0014.
Values may be sent and summed in bfloat16 or wider, within the bound.
A program may use at most 128 MiB of HBM per device.

```python
import jax
import jax.numpy as jnp
from jax import lax

D = 1024
ROWS_DEV = 2048
BLOCK = 512
PIECE = 512
CLUSTERS = 4
SLOTS = 24
ROWS = 262144
N_CLUS = 8
N_GRP = 16
DEVICES = 128


def draw_live(key, part):
    key = jax.random.fold_in(key, 7)
    devices = N_CLUS * N_GRP
    slot_count = N_CLUS + N_GRP
    first_key, second_key, third_key = jax.random.split(key, 3)
    loaded = jax.random.randint(first_key, (devices, 1), 1, 5)
    heavy_device = jax.random.randint(third_key, (), 0, devices)
    loaded = jnp.where(jnp.arange(devices)[:, None] == heavy_device, 4, loaded)
    rolled = jax.random.randint(second_key, (devices, slot_count), 0, 4)
    return (rolled < loaded).astype(jnp.int32)


def plant(drawn, stream_key, smallest, largest):
    index_at = [jax.random.randint(jax.random.fold_in(stream_key, axis), (), 0, length) for axis, length in enumerate(drawn.shape)]
    widest = drawn.shape.index(max(drawn.shape))
    beside = index_at[:widest] + [(index_at[widest] + 1) % drawn.shape[widest]] + index_at[widest + 1:]
    return drawn.at[tuple(index_at)].set(smallest).at[tuple(beside)].set(largest)


def shard_levels(stream_key, extent, shards, least, high):
    loudness, own = 1.0, jax.random.fold_in(stream_key, 6)
    for dim, parts in shards:
        draws = jnp.exp(jax.random.uniform(jax.random.fold_in(own, dim), (parts,), jnp.float32, least / len(shards), high / len(shards)))
        loudness = loudness * jnp.repeat(draws, extent[dim] // parts).reshape([-1 if axis == dim else 1 for axis in range(len(extent))])
    return loudness


def normal_values(stream_key, extent, width, reach, pieces=(), kind=jnp.bfloat16):
    entries = jax.random.normal(stream_key, extent, jnp.float32) * width
    if len(pieces) > 0:
        entries = shard_levels(stream_key, extent, pieces, -0.22, 0.18) * entries
    return jnp.clip(entries, min=-reach, max=reach).astype(kind)


def setup_inputs(seed: int = 0) -> dict:
    key_of = jax.random.split(jax.random.key(seed), 6)
    return {
        "embeddings": normal_values(key_of[0], (ROWS, D), 1.0, 6.0, ((0, 128),)),
        "labels": plant(jax.random.randint(key_of[1], (ROWS,), 0, CLUSTERS), jax.random.fold_in(key_of[1], 1), 0, CLUSTERS - 1).astype(jnp.int32),
        "partner_block": plant(jax.random.randint(key_of[2], (DEVICES, SLOTS), 0, ROWS_DEV // PIECE), jax.random.fold_in(key_of[2], 1), 0, (ROWS_DEV // PIECE) - 1).astype(jnp.int32),
        "own_block": plant(jax.random.randint(key_of[3], (DEVICES, SLOTS), 0, ROWS_DEV // BLOCK), jax.random.fold_in(key_of[3], 1), 0, (ROWS_DEV // BLOCK) - 1).astype(jnp.int32),
        "live": draw_live(jax.random.fold_in(key_of[5], 71), 0),
    }


EPS = 1e-06
FILL = -1.0

def normalize_rows(embeddings):
    widened = embeddings.astype(jnp.float32)
    inverse = lax.rsqrt(lax.optimization_barrier(jnp.sum(widened * widened, axis=1, keepdims=True)) + EPS)
    return (widened * inverse).astype(jnp.bfloat16)

def score_pair(own_rows, own_ids, own_labs, part_rows, part_ids, part_labs, active):
    cosine = jnp.dot(own_rows, part_rows.T, preferred_element_type=jnp.float32)
    keep_mask = (own_labs[:, None] == part_labs[None, :]) & (own_ids[:, None] != part_ids[None, :]) & (active > 0)
    scored = jnp.where(keep_mask, cosine, FILL)
    return (lax.optimization_barrier(jnp.max(scored, axis=1)), lax.optimization_barrier(jnp.max(scored, axis=0)))

def raise_rows(best_now, values, anchor):
    length = values.shape[0]
    current = lax.dynamic_slice_in_dim(best_now, anchor, length, 0)
    return lax.dynamic_update_slice_in_dim(best_now, jnp.maximum(current, values), anchor, 0)

def reference(embeddings, labels, partner_block, own_block, live):
    normed = normalize_rows(embeddings)
    slot_count = N_CLUS + N_GRP
    visits = N_CLUS * N_GRP * slot_count
    best_sim = jnp.full((embeddings.shape[0],), FILL, jnp.float32)

    def visit(counter, best_now):
        counter = jnp.asarray(counter).astype(jnp.int32)
        device = counter // slot_count
        slot_at = counter % slot_count
        clus_pos = device // N_GRP
        grp_pos = device % N_GRP
        partner = jnp.where(slot_at < N_CLUS, slot_at * N_GRP + grp_pos, clus_pos * N_GRP + slot_at - N_CLUS).astype(jnp.int32)
        own_anchor = (device * ROWS_DEV + own_block[device, slot_at] * BLOCK).astype(jnp.int32)
        part_anchor = (partner * ROWS_DEV + partner_block[device, slot_at] * PIECE).astype(jnp.int32)
        own_rows = lax.dynamic_slice_in_dim(normed, own_anchor, BLOCK, 0)
        part_rows = lax.dynamic_slice_in_dim(normed, part_anchor, PIECE, 0)
        own_labs = lax.dynamic_slice_in_dim(labels, own_anchor, BLOCK, 0)
        part_labs = lax.dynamic_slice_in_dim(labels, part_anchor, PIECE, 0)
        own_ids = own_anchor + jnp.arange(BLOCK, dtype=jnp.int32)
        part_ids = part_anchor + jnp.arange(PIECE, dtype=jnp.int32)
        row_best, col_best = score_pair(own_rows, own_ids, own_labs, part_rows, part_ids, part_labs, live[device, slot_at])
        best_now = raise_rows(best_now, row_best, own_anchor)
        return raise_rows(best_now, col_best, part_anchor)
    return lax.fori_loop(0, visits, visit, best_sim)
```

```python
import jax
import jax.numpy as jnp
from jax import lax
from jax.experimental import pallas as pl
from jax.experimental.pallas import tpu as pltpu
from jax.sharding import PartitionSpec as P

MESH = pl.DeviceIdType.MESH
ROWS = 2048
D = 1024
BLOCK = 512
BLOCKS = ROWS // BLOCK
EPS = 1e-06
FILL = -1.0

PIECE = 256
PIECES = ROWS // PIECE
CHUNK = 128
CHUNKS = ROWS // CHUNK
PER = PIECE // CHUNK

EE_HUB = [(0, 0, 0), (0, 0, 2), (0, 1, 0), (0, 1, 1), (0, 2, 0), (0, 3, 0), (2, 3, 0), (1, 2, 0), (1, 2, 1),
          (1, 3, 0), (1, 3, 1), (0, 4, 0), (0, 4, 1), (1, 4, 0), (1, 4, 1), (3, 4, 0), (3, 4, 1)]
EL_HUB = [(1, 0, 0), (1, 1, 0), (2, 1, 0), (2, 1, 1), (3, 2, 0), (3, 2, 1), (4, 1, 0), (4, 1, 1),
          (0, 2, 0), (0, 2, 1), (1, 2, 0), (1, 2, 1)]
LL_HUB = [(0, 1, 0), (1, 2, 0), (1, 2, 1)]
EE_CLUS = [(0, 0, 0), (0, 0, 2), (0, 1, 0), (0, 1, 1)]
EL_CLUS = [(0, 2, 0), (0, 2, 1), (0, 3, 0), (0, 3, 1), (1, 2, 0), (1, 2, 1), (1, 3, 0), (1, 3, 1)]
LL_CLUS = [(0, 2, 0), (0, 3, 0), (1, 2, 0), (1, 3, 0)]
PLACE_A = [(0, 0), (0, 3), (3, 0), (1, 0), (3, 1), (3, 3), (1, 3), (3, 2), (0, 0)]
PLACE_B = [(0, 0), (0, 1), (3, 0), (1, 0), (0, 3), (3, 1), (1, 1), (0, 2), (0, 0)]
PLACE_C = [(0, 0), (0, 1), (0, 0), (0, 0), (0, 0), (3, 1), (3, 0), (1, 1), (1, 0)]
LATE = 5
WORD = 9


def packed(values, bits):
    words = [0, 0]
    for at, value in enumerate(values):
        words[at // WORD] |= value << bits * (at % WORD)
    return words


def flags(values):
    return sum(int(value) << at for at, value in enumerate(values))


def kernel(emb, labs, own_tab, part_tab, live_tab, out, early, late, meta_e, meta_l, tabs, best, ret,
           in_sem, tab_sem, own_send, fwd_send, meta_send, ret_send,
           e1_recv, e2_recv, l0_recv, one_recv, x_recv, meta_recv, ret_recv):
    c = lax.axis_index("clus")
    g = lax.axis_index("grp")
    x, k = c // 2, c % 2
    z, y = g // 4, g % 4
    yy = (y + 2 * k) % 4
    hub = yy < 2
    hub_f = 1 - yy // 2
    is_a, is_b = yy == 0, yy == 1
    kc = 1 - y // 2

    def dev(dx, core, dz, dy):
        return (((x + dx) % 4) * 2 + core, ((z + dz) % 4) * 4 + (y + dy) % 4)

    up, down = dev(0, k, 1, 0), dev(0, k, 3, 0)
    mate = dev(0, 1 - k, 0, 0)
    x_up, x_down = dev(1, kc, 0, 0), dev(3, kc, 0, 0)
    beside = dev(0, k, 0, 1 + 2 * ((yy + 1) // 2 % 2))

    barrier = pltpu.get_barrier_semaphore()

    def greet(device):
        pl.semaphore_signal(barrier, inc=1, device_id=device, device_id_type=MESH)

    for device in (x_up, x_down, mate):
        greet(device)

    @pl.when(is_a)
    def _():
        for dz, dy in ((1, 0), (3, 0), (0, 1), (3, 1), (0, 3), (1, 3), (3, 3), (3, 2)):
            greet(dev(0, k, dz, dy))

    @pl.when(is_b)
    def _():
        for dz, dy in ((1, 0), (3, 0), (0, 3), (1, 3), (0, 1), (1, 1), (3, 1), (0, 2)):
            greet(dev(0, k, dz, dy))

    @pl.when(yy == 3)
    def _():
        for dz, dy in ((0, 1), (1, 1), (3, 1), (0, 2)):
            greet(dev(0, k, dz, dy))

    @pl.when(yy == 2)
    def _():
        for dz, dy in ((0, 3), (1, 3), (3, 3), (1, 2)):
            greet(dev(0, k, dz, dy))

    @pl.when(hub_f == 0)
    def _():
        for dx in (1, 3):
            greet(dev(dx, 1 - k, 0, 0))

    def part_of(ref, item, at, size):
        per = BLOCK // size
        return ref.at[item, at // per, pl.ds(pl.multiple_of(at % per * size, size), size)]

    def piece_of(ref, item, p):
        return part_of(ref, item, p, PIECE)

    def chunk_of(ref, item, chunk):
        return part_of(ref, item, chunk, CHUNK)

    def piece_in(p):
        return pltpu.make_async_copy(emb.at[pl.ds(p * PIECE, PIECE)], piece_of(early, 0, p), in_sem.at[p])

    for p in range(PIECES):
        piece_in(p).start()
    for b in range(BLOCKS):
        meta_e[0, b, 0:4, :] = labs[4 * b:4 * b + 4, :]
    for at, tab in enumerate((own_tab, part_tab, live_tab)):
        meta_e[0, BLOCKS, at:at + 1, 0:24] = tab[...]

    def remote(src, dst, send, recv, device):
        return pltpu.make_async_remote_copy(src_ref=src, dst_ref=dst, send_sem=send, recv_sem=recv,
                                            device_id=device, device_id_type=MESH)

    def arrived(ref, sem):
        pltpu.make_async_copy(ref, ref, sem).wait()

    def meta_copy(src, dst, item, send, device):
        return remote(src, dst, meta_send.at[send], meta_recv.at[item], device)

    def normalize(p):
        piece_in(p).wait()
        rows = piece_of(early, 0, p)
        wide = rows[...].astype(jnp.float32)
        inverse = lax.rsqrt(jnp.sum(wide * wide, axis=1, keepdims=True) + EPS)
        rows[...] = (wide * inverse).astype(jnp.bfloat16)

    normalize(0)
    pl.semaphore_wait(barrier, 9 + 2 * hub_f)

    x_from = 1 - hub_f
    meta_copy(meta_e.at[0], meta_l.at[x_from], LATE + x_from, 0, x_up).start()
    meta_copy(meta_e.at[0], meta_l.at[2 + x_from], LATE + 2 + x_from, 1, x_down).start()

    @pl.when(hub)
    def _():
        meta_copy(meta_e.at[0], meta_e.at[2], 2, 2, up).start()
        meta_copy(meta_e.at[0], meta_e.at[3], 3, 3, down).start()
        meta_copy(meta_e.at[0], meta_e.at[1], 1, 4, mate).start()

        @pl.when(is_a)
        def _():
            meta_copy(meta_e.at[0], meta_e.at[4], 4, 5, beside).start()

    @pl.when(hub_f == 0)
    def _():
        meta_copy(meta_e.at[0], meta_e.at[1], 1, 2, beside).start()

    def send_own(p):
        piece = piece_of(early, 0, p)
        remote(piece, piece_of(late, x_from, p), own_send.at[0], x_recv.at[x_from], x_up).start()
        remote(piece, piece_of(late, 2 + x_from, p), own_send.at[1], x_recv.at[2 + x_from], x_down).start()

        def part(q, carry):
            chunk = p * PER + q
            src = chunk_of(early, 0, chunk)

            @pl.when(hub)
            def _():
                remote(src, chunk_of(early, 2, chunk), own_send.at[2], e2_recv.at[chunk], up).start()
                remote(src, chunk_of(early, 3, chunk), own_send.at[3], one_recv.at[0], down).start()

                @pl.when(is_a)
                def _():
                    remote(src, chunk_of(early, 4, chunk), own_send.at[4], one_recv.at[1], beside).start()

            @pl.when(hub_f == 0)
            def _():
                remote(src, chunk_of(early, 1, chunk), own_send.at[2], e1_recv.at[chunk], beside).start()
            return carry

        lax.fori_loop(0, PER, part, 0)

        @pl.when(hub)
        def _():
            remote(piece, piece_of(early, 1, p), own_send.at[5], one_recv.at[4], mate).start()

    send_own(0)

    def rest(p, carry):
        normalize(p)
        send_own(p)
        return carry

    lax.fori_loop(1, PIECES, rest, 0)

    @pl.when(hub)
    def _():
        arrived(meta_e.at[1], meta_recv.at[1])
        meta_copy(meta_e.at[1], meta_l.at[0], LATE, 6, up).start()
        meta_copy(meta_e.at[1], meta_l.at[1], LATE + 1, 7, down).start()

        @pl.when(is_a)
        def _():
            meta_copy(meta_e.at[1], meta_l.at[2], LATE + 2, 8, beside).start()

        arrived(meta_e.at[2], meta_recv.at[2])

        @pl.when(is_b)
        def _():
            meta_copy(meta_e.at[2], meta_e.at[4], 4, 5, beside).start()

        def take(chunk, carry):
            src = chunk_of(early, 1, chunk)
            arrived(src, e1_recv.at[chunk])
            remote(src, chunk_of(late, 0, chunk), fwd_send.at[0], l0_recv.at[chunk], up).start()
            remote(src, chunk_of(late, 1, chunk), fwd_send.at[1], one_recv.at[2], down).start()

            @pl.when(is_a)
            def _():
                remote(src, chunk_of(late, 2, chunk), fwd_send.at[2], one_recv.at[3], beside).start()

            arrived(chunk_of(early, 2, chunk), e2_recv.at[chunk])

            @pl.when(is_b)
            def _():
                remote(chunk_of(early, 2, chunk), chunk_of(early, 4, chunk), own_send.at[4], one_recv.at[1], beside).start()
            return carry

        lax.fori_loop(0, CHUNKS, take, 0)
        arrived(meta_l.at[0], meta_recv.at[LATE])

        @pl.when(is_b)
        def _():
            meta_copy(meta_l.at[0], meta_l.at[2], LATE + 2, 8, beside).start()

        arrived(early.at[3], one_recv.at[0])
        arrived(early.at[4], one_recv.at[1])
        for item in (3, 4):
            arrived(meta_e.at[item], meta_recv.at[item])
        for item in (1, 2):
            arrived(meta_l.at[item], meta_recv.at[LATE + item])

    @pl.when(hub_f == 0)
    def _():
        arrived(early.at[1], one_recv.at[4])
        arrived(meta_e.at[1], meta_recv.at[1])
        for item in range(4):
            arrived(meta_l.at[item], meta_recv.at[LATE + item])

    copies = [pltpu.make_async_copy(meta_e.at[item, BLOCKS], tabs.at[item], tab_sem.at[item]) for item in range(5)]
    copies += [pltpu.make_async_copy(meta_l.at[item, BLOCKS], tabs.at[LATE + item], tab_sem.at[LATE + item])
               for item in range(4)]
    for copy in copies:
        copy.start()
    for copy in copies:
        copy.wait()

    best[...] = jnp.full(best.shape, FILL, jnp.float32)

    def by_role(for_hub, for_clus):
        return for_clus + (for_hub - for_clus) * hub_f

    def lists(for_hub, for_clus):
        fields = []
        for f in range(2):
            ours, theirs = packed([e[f] for e in for_hub], 3), packed([e[f] for e in for_clus], 3)
            fields.append([by_role(ours[w], theirs[w]) for w in range(2)])
        return fields + [by_role(flags([e[2] == 1 for e in for_hub]), flags([e[2] == 1 for e in for_clus]))]

    todo = (lists(EE_HUB, EE_CLUS), lists(EL_HUB, EL_CLUS), lists(LL_HUB, LL_CLUS))
    offsets = []
    for f in range(2):
        a, b, c_ = (packed([p[f] for p in place], 2)[0] for place in (PLACE_A, PLACE_B, PLACE_C))
        offsets.append(by_role(a + (b - a) * (yy % 2), c_))

    item_at = lax.broadcasted_iota(jnp.int32, best.shape, 0)
    block_at = lax.broadcasted_iota(jnp.int32, best.shape, 1) // 4

    def pair(kind, at):
        second_word = at // WORD
        shift = 3 * (at - WORD * second_word)
        row, col = (((words[0] + (words[1] - words[0]) * second_word) >> shift) & 7 for words in todo[kind][:2])
        asks = (todo[kind][2] >> at) & 1
        row_item = row + (LATE if kind == 2 else 0)
        col_item = col + (LATE if kind > 0 else 0)
        asker = row_item + (col_item - row_item) * asks
        other = row_item + col_item - asker
        first, second = ((offset >> (2 * other)) & 3 for offset in offsets)
        row_ref, row_meta = (late, meta_l) if kind == 2 else (early, meta_e)
        col_ref, col_meta = (late, meta_l) if kind > 0 else (early, meta_e)
        place_c = ((x + first) % 4) * 2 + (k + second) % 2
        place_g = 8 + ((z + first) % 4) * 4 + (y + second) % 4
        in_grp = hub_f
        if kind == 0:
            own_pair = 1 - jnp.minimum(at // 2, 1)
            in_grp = own_pair * at + (1 - own_pair) * hub_f
        place = in_grp * place_g + (1 - in_grp) * place_c
        row_block = tabs[asker, asks, place]
        col_block = tabs[asker, 1 - asks, place]
        alive = tabs[asker, 2, place]
        rows = row_ref[row, row_block]
        row_labs = [row_meta[row, row_block, i:i + 1, :].astype(jnp.float32) for i in range(4)]
        col_labs = [col_meta[col, col_block, i:i + 1, :].astype(jnp.float32) for i in range(4)]
        row_labs = [jnp.transpose(jnp.broadcast_to(lab, (128, 128))) for lab in row_labs]
        row_best = [None] * 4
        col_best = [None] * 4
        if kind == 0:
            apart = jnp.where((row == col) & (row_block == col_block), 0, 1)
            off = (lax.broadcasted_iota(jnp.int32, (128, 128), 0) != lax.broadcasted_iota(jnp.int32, (128, 128), 1))
            off = off | (jnp.full((128, 128), apart, jnp.int32) > 0)
        half = BLOCK // 2
        for n in range(2):
            cols = col_ref[col, col_block, n * half:(n + 1) * half, :]
            cosine = lax.dot_general(rows, cols, (((1,), (1,)), ((), ())), preferred_element_type=jnp.float32)
            for jj in range(2):
                j = 2 * n + jj
                for i in range(4):
                    tile = cosine[i * 128:(i + 1) * 128, jj * 128:(jj + 1) * 128]
                    keep = row_labs[i] == col_labs[j]
                    if kind == 0 and i == j:
                        keep = keep & off
                    tile = jnp.where(keep, tile, FILL)
                    row_best[i] = tile if row_best[i] is None else jnp.maximum(row_best[i], tile)
                    folded = jnp.max(tile.reshape(16, 8, 128), axis=0)
                    col_best[j] = folded if col_best[j] is None else jnp.maximum(col_best[j], folded)
        row_best = jnp.concatenate([jnp.max(jnp.transpose(t), axis=0, keepdims=True) for t in row_best] * 4, axis=0)
        col_best = jnp.concatenate([jnp.max(t, axis=0, keepdims=True) for t in col_best] * 4, axis=0)
        now = best[...]
        for values, item, block in ((row_best, row_item, row_block), (col_best, col_item, col_block)):
            hit = (item_at == item) & (block_at == block) & (jnp.full(best.shape, alive, jnp.int32) > 0)
            now = jnp.maximum(now, jnp.where(hit, values[None], FILL))
        best[...] = now

    def first_step(at, carry):
        @pl.when(hub & (at < CHUNKS))
        def _():
            src = chunk_of(late, 0, at)
            arrived(src, l0_recv.at[at])

            @pl.when(is_b)
            def _():
                remote(src, chunk_of(late, 2, at), fwd_send.at[2], one_recv.at[3], beside).start()
        pair(0, at)
        return carry

    lax.fori_loop(0, len(EE_CLUS) + (len(EE_HUB) - len(EE_CLUS)) * hub_f, first_step, 0)

    @pl.when(hub)
    def _():
        arrived(late.at[1], one_recv.at[2])
        arrived(late.at[2], one_recv.at[3])

    @pl.when(hub_f == 0)
    def _():
        for item in range(4):
            arrived(late.at[item], x_recv.at[item])

    def second_step(at, carry):
        pair(1, at)
        return carry

    def third_step(at, carry):
        pair(2, at)
        return carry

    lax.fori_loop(0, len(EL_CLUS) + (len(EL_HUB) - len(EL_CLUS)) * hub_f, second_step, 0)
    lax.fori_loop(0, len(LL_CLUS) + (len(LL_HUB) - len(LL_CLUS)) * hub_f, third_step, 0)

    def give(item, to, send, device):
        return remote(best.at[item], ret.at[to], ret_send.at[send], ret_recv.at[to], device)

    def hub_gives(a):
        return [give(1, 0, 0, dev(0, k, 0, 3 if a else 1)), give(2, 0, 1, dev(0, k, 3, 0)), give(3, 1, 2, dev(0, k, 1, 0)),
                give(4, 2, 3, dev(0, k, 3, 1) if a else dev(0, k, 0, 3)),
                give(5, 1, 4, dev(0, k, 3, 3 if a else 1)), give(6, 2, 5, dev(0, k, 1, 3 if a else 1)),
                give(7, 3, 6, dev(0, k, 3, 2) if a else dev(0, k, 0, 2))]

    def clus_gives():
        return [give(1, 3, 0, mate), give(5, 4, 1, dev(3, 1 - k, 0, 0)), give(6, 4, 2, dev(3, k, 0, 0)),
                give(7, 5, 3, dev(1, 1 - k, 0, 0)), give(8, 5, 4, dev(1, k, 0, 0))]

    for which, gives in ((is_a, lambda: hub_gives(True)), (is_b, lambda: hub_gives(False)), (hub_f == 0, clus_gives)):
        @pl.when(which)
        def _(gives=gives):
            for copy in gives():
                copy.start()

    for s in range(2):
        arrived(early.at[0], own_send.at[s])
        arrived(meta_e.at[0], meta_send.at[s])

    @pl.when(hub)
    def _():
        for s in range(2, 6):
            arrived(early.at[0], own_send.at[s])
        for s in range(3):
            arrived(early.at[0], fwd_send.at[s])
        for s in range(2, 9):
            arrived(meta_e.at[0], meta_send.at[s])
        for s in range(7):
            arrived(best.at[0], ret_send.at[s])

    @pl.when(hub_f == 0)
    def _():
        arrived(early.at[0], own_send.at[2])
        arrived(meta_e.at[0], meta_send.at[2])
        for s in range(5):
            arrived(best.at[0], ret_send.at[s])

    result = best[0]
    for j in range(6):
        arrived(ret.at[j], ret_recv.at[j])
        result = jnp.maximum(result, ret[j])
    out[...] = result


def on_device(embeddings, labels, partner_block, own_block, live):
    dma = pltpu.SemaphoreType.DMA
    vmem = pl.BlockSpec(memory_space=pltpu.VMEM)
    best = pl.pallas_call(
        kernel,
        out_shape=jax.ShapeDtypeStruct((16, 128), jnp.float32),
        in_specs=[pl.BlockSpec(memory_space=pl.ANY), vmem, vmem, vmem, vmem],
        out_specs=vmem,
        scratch_shapes=[
            pltpu.VMEM((5, BLOCKS, BLOCK, D), jnp.bfloat16),
            pltpu.VMEM((4, BLOCKS, BLOCK, D), jnp.bfloat16),
            pltpu.VMEM((5, BLOCKS + 1, 8, 128), jnp.int32),
            pltpu.VMEM((4, BLOCKS + 1, 8, 128), jnp.int32),
            pltpu.SMEM((9, 8, 128), jnp.int32),
            pltpu.VMEM((9, 16, 128), jnp.float32),
            pltpu.VMEM((6, 16, 128), jnp.float32),
            dma((PIECES,)), dma((9,)), dma((6,)), dma((3,)), dma((9,)), dma((7,)),
            dma((CHUNKS,)), dma((CHUNKS,)), dma((CHUNKS,)), dma((5,)), dma((4,)), dma((9,)), dma((6,)),
        ],
        compiler_params=pltpu.CompilerParams(collective_id=0, has_side_effects=True, vmem_limit_bytes=56 << 20),
        cost_estimate=pl.CostEstimate(flops=24 * 2 * 512 * 512 * 1024, bytes_accessed=4 << 20, transcendentals=2048),
    )(embeddings, labels.reshape(16, 128), own_block, partner_block, live)
    return best.reshape(2048)


def solution(mesh):
    placed = (
        P(("clus", "grp"), None),
        P(("clus", "grp")),
        P(("clus", "grp"), None),
        P(("clus", "grp"), None),
        P(("clus", "grp"), None),
    )
    return jax.shard_map(
        on_device, mesh=mesh, in_specs=placed, out_specs=P(("clus", "grp")), check_vma=False
    )
```

```python
import jax
import jax.numpy as jnp
from jax import lax
from jax.experimental import pallas as pl
from jax.experimental.pallas import tpu as pltpu
from jax.sharding import PartitionSpec as P

MESH = pl.DeviceIdType.MESH
ROWS = 2048
D = 1024
BLOCK = 512
BLOCKS = ROWS // BLOCK
EPS = 1e-06
FILL = -1.0

PIECE = 256
PIECES = ROWS // PIECE
CHUNK = 128
CHUNKS = ROWS // CHUNK
PER = PIECE // CHUNK

EE_HUB = [(0, 0, 0), (0, 0, 0), (0, 1, 0), (0, 1, 1), (0, 2, 0), (0, 3, 0), (2, 3, 0), (1, 2, 0), (1, 2, 1),
          (1, 3, 0), (1, 3, 1), (0, 4, 0), (0, 4, 1), (1, 4, 0), (1, 4, 1), (3, 4, 0), (3, 4, 1), (3, 4, 1)]
EL_HUB = [(1, 0, 0), (1, 1, 0), (2, 1, 0), (2, 1, 1), (4, 1, 0), (4, 1, 1), (3, 2, 0), (3, 2, 1),
          (0, 2, 0), (0, 2, 1), (1, 2, 0), (1, 2, 1)]
LL_HUB = [(0, 1, 0), (1, 2, 0), (1, 2, 1), (1, 2, 1)]
EE_CLUS = [(0, 0, 0), (0, 0, 0), (0, 1, 0), (0, 1, 1)]
EL_CLUS = [(0, 2, 0), (0, 2, 1), (1, 2, 0), (1, 2, 1), (0, 3, 0), (0, 3, 1), (1, 3, 0), (1, 3, 1),
           (0, 2, 0), (0, 2, 1), (1, 2, 0), (1, 2, 1)]
LL_CLUS = [(0, 2, 0), (0, 3, 0), (1, 2, 0), (1, 3, 0)]
PLACE_A = [(0, 0), (0, 3), (3, 0), (1, 0), (3, 1), (3, 3), (1, 3), (3, 2), (0, 0)]
PLACE_B = [(0, 0), (0, 1), (3, 0), (1, 0), (0, 3), (3, 1), (1, 1), (0, 2), (0, 0)]
PLACE_C = [(0, 0), (0, 1), (0, 0), (0, 0), (0, 0), (3, 1), (3, 0), (1, 1), (1, 0)]
LATE = 5
WORD = 9


def packed(values, bits):
    words = [0, 0]
    for at, value in enumerate(values):
        words[at // WORD] |= value << bits * (at % WORD)
    return words


def flags(values):
    return sum(int(value) << at for at, value in enumerate(values))


def kernel(emb, labs, own_tab, part_tab, live_tab, out, early, late, meta_e, meta_l, tabs, best, ret,
           in_sem, tab_sem, own_send, fwd_send, meta_send, ret_send,
           e1_recv, e2_recv, late_recv, one_recv, meta_recv, ret_recv):
    c = lax.axis_index("clus")
    g = lax.axis_index("grp")
    x, k = c // 2, c % 2
    z, y = g // 4, g % 4
    yy = (y + 2 * k) % 4
    hub = yy < 2
    hub_f = 1 - yy // 2
    is_a, is_b = yy == 0, yy == 1
    kc = 1 - y // 2

    def dev(dx, core, dz, dy):
        return (((x + dx) % 4) * 2 + core, ((z + dz) % 4) * 4 + (y + dy) % 4)

    up, down = dev(0, k, 1, 0), dev(0, k, 3, 0)
    mate = dev(0, 1 - k, 0, 0)
    x_up, x_down = dev(1, kc, 0, 0), dev(3, kc, 0, 0)
    beside = dev(0, k, 0, 1 + 2 * ((yy + 1) // 2 % 2))

    barrier = pltpu.get_barrier_semaphore()

    def greet(*devices):
        for device in devices:
            pl.semaphore_signal(barrier, inc=1, device_id=device, device_id_type=MESH)

    @pl.when(hub)
    def _():
        greet(up, down, beside, dev(0, k, 0, 3 - 2 * (yy % 2)))

    @pl.when(hub_f == 0)
    def _():
        greet(mate, x_up, x_down, dev(1, 1 - k, 0, 0), dev(3, 1 - k, 0, 0))

    def part_of(ref, item, at, size):
        per = BLOCK // size
        return ref.at[item, at // per, pl.ds(pl.multiple_of(at % per * size, size), size)]

    def piece_of(ref, item, p):
        return part_of(ref, item, p, PIECE)

    def chunk_of(ref, item, chunk):
        return part_of(ref, item, chunk, CHUNK)

    def piece_in(p):
        return pltpu.make_async_copy(emb.at[pl.ds(p * PIECE, PIECE)], piece_of(early, 0, p), in_sem.at[p])

    for p in range(PIECES):
        piece_in(p).start()
    for b in range(BLOCKS):
        meta_e[0, b, 0:4, :] = labs[4 * b:4 * b + 4, :]
    for at, tab in enumerate((own_tab, part_tab, live_tab)):
        meta_e[0, BLOCKS, at:at + 1, 0:24] = tab[...]

    def remote(src, dst, send, recv, device):
        return pltpu.make_async_remote_copy(src_ref=src, dst_ref=dst, send_sem=send, recv_sem=recv,
                                            device_id=device, device_id_type=MESH)

    def arrived(ref, sem):
        pltpu.make_async_copy(ref, ref, sem).wait()

    def meta_copy(src, dst, item, send, device):
        return remote(src, dst, meta_send.at[send], meta_recv.at[item], device)

    def normalize(p):
        piece_in(p).wait()
        rows = piece_of(early, 0, p)
        wide = rows[...].astype(jnp.float32)
        inverse = lax.rsqrt(jnp.sum(wide * wide, axis=1, keepdims=True) + EPS)
        rows[...] = (wide * inverse).astype(jnp.bfloat16)

    normalize(0)
    pl.semaphore_wait(barrier, 3 + 3 * hub_f)

    x_from = 1 - hub_f
    meta_copy(meta_e.at[0], meta_l.at[x_from], LATE + x_from, 0, x_up).start()
    meta_copy(meta_e.at[0], meta_l.at[2 + x_from], LATE + 2 + x_from, 1, x_down).start()

    @pl.when(hub)
    def _():
        meta_copy(meta_e.at[0], meta_e.at[2], 2, 2, up).start()
        meta_copy(meta_e.at[0], meta_e.at[3], 3, 3, down).start()
        meta_copy(meta_e.at[0], meta_e.at[1], 1, 4, mate).start()

        @pl.when(is_a)
        def _():
            meta_copy(meta_e.at[0], meta_e.at[4], 4, 5, beside).start()

    @pl.when(hub_f == 0)
    def _():
        meta_copy(meta_e.at[0], meta_e.at[1], 1, 2, beside).start()

    def send_own(p):
        piece = piece_of(early, 0, p)
        remote(piece, piece_of(late, x_from, p), own_send.at[0], late_recv.at[x_from, p], x_up).start()
        remote(piece, piece_of(late, 2 + x_from, p), own_send.at[1], late_recv.at[2 + x_from, p], x_down).start()

        def part(q, carry):
            chunk = p * PER + q
            src = chunk_of(early, 0, chunk)

            @pl.when(hub)
            def _():
                remote(src, chunk_of(early, 2, chunk), own_send.at[2], e2_recv.at[chunk], up).start()
                remote(src, chunk_of(early, 3, chunk), own_send.at[3], one_recv.at[0], down).start()

                @pl.when(is_a)
                def _():
                    remote(src, chunk_of(early, 4, chunk), own_send.at[4], one_recv.at[1], beside).start()

            @pl.when(hub_f == 0)
            def _():
                remote(src, chunk_of(early, 1, chunk), own_send.at[2], e1_recv.at[chunk], beside).start()
            return carry

        lax.fori_loop(0, PER, part, 0)

        @pl.when(hub)
        def _():
            remote(piece, piece_of(early, 1, p), own_send.at[5], one_recv.at[2], mate).start()

    send_own(0)

    def rest(p, carry):
        normalize(p)
        send_own(p)
        return carry

    lax.fori_loop(1, PIECES, rest, 0)

    @pl.when(hub)
    def _():
        arrived(meta_e.at[1], meta_recv.at[1])
        meta_copy(meta_e.at[1], meta_l.at[0], LATE, 6, up).start()
        meta_copy(meta_e.at[1], meta_l.at[1], LATE + 1, 7, down).start()

        @pl.when(is_a)
        def _():
            meta_copy(meta_e.at[1], meta_l.at[2], LATE + 2, 8, beside).start()

        arrived(meta_e.at[2], meta_recv.at[2])

        @pl.when(is_b)
        def _():
            meta_copy(meta_e.at[2], meta_e.at[4], 4, 5, beside).start()

        def take(chunk, carry):
            src = chunk_of(early, 1, chunk)
            arrived(src, e1_recv.at[chunk])
            remote(src, chunk_of(late, 0, chunk), fwd_send.at[0], late_recv.at[0, chunk], up).start()
            remote(src, chunk_of(late, 1, chunk), fwd_send.at[1], late_recv.at[1, chunk], down).start()

            @pl.when(is_a)
            def _():
                remote(src, chunk_of(late, 2, chunk), fwd_send.at[2], late_recv.at[2, chunk], beside).start()

            arrived(chunk_of(early, 2, chunk), e2_recv.at[chunk])

            @pl.when(is_b)
            def _():
                remote(chunk_of(early, 2, chunk), chunk_of(early, 4, chunk), own_send.at[4], one_recv.at[1], beside).start()
            return carry

        lax.fori_loop(0, CHUNKS, take, 0)
        arrived(meta_l.at[0], meta_recv.at[LATE])

        @pl.when(is_b)
        def _():
            meta_copy(meta_l.at[0], meta_l.at[2], LATE + 2, 8, beside).start()

        arrived(early.at[3], one_recv.at[0])
        arrived(early.at[4], one_recv.at[1])
        for item in (3, 4):
            arrived(meta_e.at[item], meta_recv.at[item])
        for item in (1, 2):
            arrived(meta_l.at[item], meta_recv.at[LATE + item])

    @pl.when(hub_f == 0)
    def _():
        arrived(early.at[1], one_recv.at[2])
        arrived(meta_e.at[1], meta_recv.at[1])
        for item in range(4):
            arrived(meta_l.at[item], meta_recv.at[LATE + item])

    copies = [pltpu.make_async_copy(meta_e.at[item, BLOCKS], tabs.at[item], tab_sem.at[item]) for item in range(5)]
    copies += [pltpu.make_async_copy(meta_l.at[item, BLOCKS], tabs.at[LATE + item], tab_sem.at[LATE + item])
               for item in range(4)]
    for copy in copies:
        copy.start()
    for copy in copies:
        copy.wait()

    best[...] = jnp.full(best.shape, FILL, jnp.float32)

    def by_role(for_hub, for_clus):
        return for_clus + (for_hub - for_clus) * hub_f

    def lists(for_hub, for_clus):
        fields = []
        for f in range(2):
            ours, theirs = packed([e[f] for e in for_hub], 3), packed([e[f] for e in for_clus], 3)
            fields.append([by_role(ours[w], theirs[w]) for w in range(2)])
        return fields + [by_role(flags([e[2] == 1 for e in for_hub]), flags([e[2] == 1 for e in for_clus]))]

    todo = (lists(EE_HUB, EE_CLUS), lists(EL_HUB, EL_CLUS), lists(LL_HUB, LL_CLUS))
    offsets = []
    for f in range(2):
        a, b, c_ = (packed([p[f] for p in place], 2)[0] for place in (PLACE_A, PLACE_B, PLACE_C))
        offsets.append(by_role(a + (b - a) * (yy % 2), c_))

    line = lax.broadcasted_iota(jnp.int32, (16, 128), 0)
    block_at = line // 4

    def look_up(kind, at):
        second_word = at // WORD
        shift = 3 * (at - WORD * second_word)
        row, col = (((words[0] + (words[1] - words[0]) * second_word) >> shift) & 7 for words in todo[kind][:2])
        asks = (todo[kind][2] >> at) & 1
        row_item = row + (LATE if kind == 2 else 0)
        col_item = col + (LATE if kind > 0 else 0)
        asker = row_item + (col_item - row_item) * asks
        other = row_item + col_item - asker
        first, second = ((offset >> (2 * other)) & 3 for offset in offsets)
        place_c = ((x + first) % 4) * 2 + (k + second) % 2
        place_g = 8 + ((z + first) % 4) * 4 + (y + second) % 4
        in_grp = hub_f
        if kind == 0:
            own_pair = 1 - jnp.minimum(at // 2, 1)
            in_grp = own_pair * at + (1 - own_pair) * hub_f
        place = in_grp * place_g + (1 - in_grp) * place_c
        return row, col, row_item, col_item, tabs[asker, asks, place], tabs[asker, 1 - asks, place], tabs[asker, 2, place]

    def labels_down(meta, item, block):
        labs = [meta[item, block, i:i + 1, :].astype(jnp.float32) for i in range(4)]
        return [jnp.transpose(jnp.broadcast_to(lab, (128, 128))) for lab in labs]

    def raise_best(item, values, where):
        best[item] = jnp.maximum(best[item], jnp.where(where, values, FILL))

    def full(scalar):
        return jnp.full((16, 128), scalar, jnp.int32)

    def score(rows, cols, row_labs, col_labs, off, row_best, col_best):
        cosine = lax.dot_general(rows, cols, (((1,), (1,)), ((), ())), preferred_element_type=jnp.float32)
        for j, col_lab in enumerate(col_labs):
            line_best = None
            for i in range(4):
                tile = cosine[i * 128:(i + 1) * 128, j * 128:(j + 1) * 128]
                keep = row_labs[i] == col_lab
                if off is not None and i == len(col_best):
                    keep = keep & off
                tile = jnp.where(keep, tile, FILL)
                row_best[i] = tile if row_best[i] is None else jnp.maximum(row_best[i], tile)
                folded = jnp.max(tile.reshape(16, 8, 128), axis=0)
                line_best = folded if line_best is None else jnp.maximum(line_best, folded)
            col_best.append(jnp.max(line_best, axis=0, keepdims=True))

    def down_rows(row_best):
        return jnp.concatenate([jnp.max(jnp.transpose(t), axis=0, keepdims=True) for t in row_best] * 4, axis=0)

    def pair(kind, at):
        row, col, row_item, col_item, row_block, col_block, alive = look_up(kind, at)
        row_ref, row_meta = (late, meta_l) if kind == 2 else (early, meta_e)
        col_ref, col_meta = (late, meta_l) if kind > 0 else (early, meta_e)
        rows = row_ref[row, row_block]
        row_labs = labels_down(row_meta, row, row_block)
        col_labs = [col_meta[col, col_block, i:i + 1, :].astype(jnp.float32) for i in range(4)]
        off = None
        if kind == 0:
            apart = jnp.where((row == col) & (row_block == col_block), 0, 1)
            off = (lax.broadcasted_iota(jnp.int32, (128, 128), 0) != lax.broadcasted_iota(jnp.int32, (128, 128), 1))
            off = off | (jnp.full((128, 128), apart, jnp.int32) > 0)
        row_best, col_best = [None] * 4, []
        for n in range(2):
            cols = col_ref[col, col_block, n * PIECE:(n + 1) * PIECE, :]
            score(rows, cols, row_labs, col_labs[2 * n:2 * n + 2], off, row_best, col_best)
        raise_best(row_item, down_rows(row_best), (block_at == row_block) & (full(alive) > 0))
        raise_best(col_item, jnp.concatenate(col_best * 4, axis=0), (block_at == col_block) & (full(alive) > 0))

    def late_pair(at, p):
        row, col, row_item, col_item, row_block, col_block, alive = look_up(1, at)
        block, half = p // 2, p % 2
        rows = early[row, row_block]
        row_labs = labels_down(meta_e, row, row_block)
        col_labs = [meta_l[col, block, pl.ds(half * 2 + j, 1), :].astype(jnp.float32) for j in range(2)]
        row_best, col_best = [None] * 4, []
        score(rows, piece_of(late, col, p)[...], row_labs, col_labs, None, row_best, col_best)
        asked = full(jnp.where(col_block == block, alive, 0)) > 0
        raise_best(row_item, down_rows(row_best), (block_at == row_block) & asked)
        at_line = block * 4 + half * 2
        both = jnp.where(line == at_line, col_best[0], col_best[1])
        raise_best(col_item, both, asked & ((line == at_line) | (line == at_line + 1)))

    def pass_on(chunk):
        src = chunk_of(late, 0, chunk)
        arrived(src, late_recv.at[0, chunk])

        @pl.when(is_b)
        def _():
            remote(src, chunk_of(late, 2, chunk), fwd_send.at[2], late_recv.at[2, chunk], beside).start()

    early_pairs = len(EE_CLUS) + (len(EE_HUB) - len(EE_CLUS)) * hub_f

    def step(p, carry):
        @pl.when(hub)
        def _():
            pass_on(2 * p)

        @pl.when(2 * p < early_pairs)
        def _():
            pair(0, 2 * p)
            pair(0, 2 * p + 1)

        @pl.when(hub)
        def _():
            pass_on(2 * p + 1)
            for item in (1, 2):
                for chunk in (2 * p, 2 * p + 1):
                    arrived(chunk_of(late, item, chunk), late_recv.at[item, chunk])

        @pl.when(hub_f == 0)
        def _():
            for item in range(4):
                arrived(piece_of(late, item, p), late_recv.at[item, p])

        for at in range(len(EL_HUB)):
            late_pair(at, p)
        return carry

    @pl.when(hub)
    def _():
        pair(0, 16)
        pair(0, 17)

    lax.fori_loop(0, PIECES, step, 0)
    for at in range(len(LL_HUB)):
        pair(2, at)

    def give(item, to, send, device):
        return remote(best.at[item], ret.at[to], ret_send.at[send], ret_recv.at[to], device)

    def hub_gives(a):
        return [give(1, 0, 0, dev(0, k, 0, 3 if a else 1)), give(2, 0, 1, dev(0, k, 3, 0)), give(3, 1, 2, dev(0, k, 1, 0)),
                give(4, 2, 3, dev(0, k, 3, 1) if a else dev(0, k, 0, 3)),
                give(5, 1, 4, dev(0, k, 3, 3 if a else 1)), give(6, 2, 5, dev(0, k, 1, 3 if a else 1)),
                give(7, 3, 6, dev(0, k, 3, 2) if a else dev(0, k, 0, 2))]

    def clus_gives():
        return [give(1, 3, 0, mate), give(5, 4, 1, dev(3, 1 - k, 0, 0)), give(6, 4, 2, dev(3, k, 0, 0)),
                give(7, 5, 3, dev(1, 1 - k, 0, 0)), give(8, 5, 4, dev(1, k, 0, 0))]

    for which, gives in ((is_a, lambda: hub_gives(True)), (is_b, lambda: hub_gives(False)), (hub_f == 0, clus_gives)):
        @pl.when(which)
        def _(gives=gives):
            for copy in gives():
                copy.start()

    for s in range(2):
        arrived(early.at[0], own_send.at[s])
        arrived(meta_e.at[0], meta_send.at[s])

    @pl.when(hub)
    def _():
        for s in range(2, 6):
            arrived(early.at[0], own_send.at[s])
        for s in range(3):
            arrived(early.at[0], fwd_send.at[s])
        for s in range(2, 9):
            arrived(meta_e.at[0], meta_send.at[s])
        for s in range(7):
            arrived(best.at[0], ret_send.at[s])

    @pl.when(hub_f == 0)
    def _():
        arrived(early.at[0], own_send.at[2])
        arrived(meta_e.at[0], meta_send.at[2])
        for s in range(5):
            arrived(best.at[0], ret_send.at[s])

    result = best[0]
    for j in range(6):
        arrived(ret.at[j], ret_recv.at[j])
        result = jnp.maximum(result, ret[j])
    out[...] = result


def on_device(embeddings, labels, partner_block, own_block, live):
    dma = pltpu.SemaphoreType.DMA
    vmem = pl.BlockSpec(memory_space=pltpu.VMEM)
    best = pl.pallas_call(
        kernel,
        out_shape=jax.ShapeDtypeStruct((16, 128), jnp.float32),
        in_specs=[pl.BlockSpec(memory_space=pl.ANY), vmem, vmem, vmem, vmem],
        out_specs=vmem,
        scratch_shapes=[
            pltpu.VMEM((5, BLOCKS, BLOCK, D), jnp.bfloat16),
            pltpu.VMEM((4, BLOCKS, BLOCK, D), jnp.bfloat16),
            pltpu.VMEM((5, BLOCKS + 1, 8, 128), jnp.int32),
            pltpu.VMEM((4, BLOCKS + 1, 8, 128), jnp.int32),
            pltpu.SMEM((9, 8, 128), jnp.int32),
            pltpu.VMEM((9, 16, 128), jnp.float32),
            pltpu.VMEM((6, 16, 128), jnp.float32),
            dma((PIECES,)), dma((9,)), dma((6,)), dma((3,)), dma((9,)), dma((7,)),
            dma((CHUNKS,)), dma((CHUNKS,)), dma((4, CHUNKS)), dma((3,)), dma((9,)), dma((6,)),
        ],
        compiler_params=pltpu.CompilerParams(collective_id=0, has_side_effects=True, vmem_limit_bytes=56 << 20),
        cost_estimate=pl.CostEstimate(flops=24 * 2 * 512 * 512 * 1024, bytes_accessed=4 << 20, transcendentals=2048),
    )(embeddings, labels.reshape(16, 128), own_block, partner_block, live)
    return best.reshape(2048)


def solution(mesh):
    placed = (
        P(("clus", "grp"), None),
        P(("clus", "grp")),
        P(("clus", "grp"), None),
        P(("clus", "grp"), None),
        P(("clus", "grp"), None),
    )
    return jax.shard_map(
        on_device, mesh=mesh, in_specs=placed, out_specs=P(("clus", "grp")), check_vma=False
    )
```

```python
import jax
import jax.numpy as jnp
from jax import lax
from jax.experimental import pallas as pl
from jax.experimental.pallas import tpu as pltpu
from jax.sharding import PartitionSpec as P

MESH = pl.DeviceIdType.MESH
ROWS = 2048
D = 1024
BLOCK = 512
BLOCKS = ROWS // BLOCK
EPS = 1e-06
FILL = -1.0

PIECE = 256
PIECES = ROWS // PIECE
CHUNK = 64
CHUNKS = ROWS // CHUNK
PER = PIECE // CHUNK

EE_HUB = [(0, 0, 0), (0, 0, 0), (0, 1, 0), (0, 1, 1), (0, 2, 0), (0, 3, 0), (2, 3, 0), (1, 2, 0), (1, 2, 1),
          (1, 3, 0), (1, 3, 1), (0, 4, 0), (0, 4, 1), (1, 4, 0), (1, 4, 1), (3, 4, 0), (3, 4, 1), (3, 4, 1)]
EL_HUB = [(1, 0, 0), (1, 1, 0), (2, 1, 0), (2, 1, 1), (4, 1, 0), (4, 1, 1), (3, 2, 0), (3, 2, 1),
          (0, 2, 0), (0, 2, 1), (1, 2, 0), (1, 2, 1)]
LL_HUB = [(0, 1, 0), (1, 2, 0), (1, 2, 1), (1, 2, 1), (1, 2, 1)]
EE_CLUS = [(0, 0, 0), (0, 0, 0), (0, 1, 0), (0, 1, 1)]
EL_CLUS = [(0, 1, 0), (0, 1, 1), (1, 0, 0), (1, 0, 1), (0, 1, 0), (0, 1, 1),
           (0, 2, 0), (0, 2, 1), (1, 3, 0), (1, 3, 1), (0, 2, 0), (0, 2, 1)]
LL_CLUS = [(0, 1, 0), (0, 2, 0), (0, 3, 0), (1, 2, 0), (1, 3, 0)]
EL_A = 6
PLACE_A = [(0, 0), (0, 3), (3, 0), (1, 0), (3, 1), (3, 3), (1, 3), (3, 2), (0, 0)]
PLACE_B = [(0, 0), (0, 1), (3, 0), (1, 0), (0, 3), (3, 1), (1, 1), (0, 2), (0, 0)]
PLACE_C = [(0, 0), (0, 1), (0, 0), (0, 0), (0, 0), (3, 1), (3, 0), (1, 1), (1, 0)]
LATE = 5
WORD = 9


def packed(values, bits):
    words = [0, 0]
    for at, value in enumerate(values):
        words[at // WORD] |= value << bits * (at % WORD)
    return words


def flags(values):
    return sum(int(value) << at for at, value in enumerate(values))


def kernel(emb, labs, own_tab, part_tab, live_tab, out, early, late_a, late_b, meta_e, meta_l, tabs, best, ret,
           in_sem, tab_sem, own_send, fwd_send, meta_send, ret_send,
           e1_recv, e2_recv, l0_recv, late_recv, one_recv, meta_recv, ret_recv):
    c = lax.axis_index("clus")
    g = lax.axis_index("grp")
    x, k = c // 2, c % 2
    z, y = g // 4, g % 4
    yy = (y + 2 * k) % 4
    hub = yy < 2
    hub_f = 1 - yy // 2
    is_a, is_b = yy == 0, yy == 1
    kc = 1 - y // 2

    def dev(dx, core, dz, dy):
        return (((x + dx) % 4) * 2 + core, ((z + dz) % 4) * 4 + (y + dy) % 4)

    up, down = dev(0, k, 1, 0), dev(0, k, 3, 0)
    mate = dev(0, 1 - k, 0, 0)
    x_up, x_down = dev(1, kc, 0, 0), dev(3, kc, 0, 0)
    beside = dev(0, k, 0, 1 + 2 * ((yy + 1) // 2 % 2))

    barrier = pltpu.get_barrier_semaphore()

    def greet(*devices):
        for device in devices:
            pl.semaphore_signal(barrier, inc=1, device_id=device, device_id_type=MESH)

    @pl.when(hub)
    def _():
        greet(up, down, beside, dev(0, k, 0, 3 - 2 * (yy % 2)))

    @pl.when(hub_f == 0)
    def _():
        greet(mate, x_up, x_down, dev(1, 1 - k, 0, 0), dev(3, 1 - k, 0, 0))

    def part_of(ref, item, at, size):
        per = BLOCK // size
        return ref.at[item, at // per, pl.ds(pl.multiple_of(at % per * size, size), size)]

    def piece_of(ref, item, p):
        return part_of(ref, item, p, PIECE)

    def chunk_of(ref, item, chunk):
        return part_of(ref, item, chunk, CHUNK)

    def piece_in(p):
        return pltpu.make_async_copy(emb.at[pl.ds(p * PIECE, PIECE)], piece_of(early, 0, p), in_sem.at[p])

    for p in range(PIECES):
        piece_in(p).start()
    for b in range(BLOCKS):
        meta_e[0, b, 0:4, :] = labs[4 * b:4 * b + 4, :]
    for at, tab in enumerate((own_tab, part_tab, live_tab)):
        meta_e[0, BLOCKS, at:at + 1, 0:24] = tab[...]

    def remote(src, dst, send, recv, device):
        return pltpu.make_async_remote_copy(src_ref=src, dst_ref=dst, send_sem=send, recv_sem=recv,
                                            device_id=device, device_id_type=MESH)

    def arrived(ref, sem):
        pltpu.make_async_copy(ref, ref, sem).wait()

    def meta_copy(src, dst, item, send, device):
        return remote(src, dst, meta_send.at[send], meta_recv.at[item], device)

    def normalize(p):
        piece_in(p).wait()
        rows = piece_of(early, 0, p)
        wide = rows[...].astype(jnp.float32)
        inverse = lax.rsqrt(jnp.sum(wide * wide, axis=1, keepdims=True) + EPS)
        rows[...] = (wide * inverse).astype(jnp.bfloat16)

    normalize(0)
    pl.semaphore_wait(barrier, 3 + 3 * hub_f)

    x_from = 1 - hub_f
    meta_copy(meta_e.at[0], meta_l.at[x_from], LATE + x_from, 0, x_up).start()
    meta_copy(meta_e.at[0], meta_l.at[2 + x_from], LATE + 2 + x_from, 1, x_down).start()

    @pl.when(hub)
    def _():
        meta_copy(meta_e.at[0], meta_e.at[2], 2, 2, up).start()
        meta_copy(meta_e.at[0], meta_e.at[3], 3, 3, down).start()
        meta_copy(meta_e.at[0], meta_e.at[1], 1, 4, mate).start()

        @pl.when(is_a)
        def _():
            meta_copy(meta_e.at[0], meta_e.at[4], 4, 5, beside).start()

    @pl.when(hub_f == 0)
    def _():
        meta_copy(meta_e.at[0], meta_e.at[1], 1, 2, beside).start()

    def send_own(p):
        piece = piece_of(early, 0, p)

        @pl.when(hub)
        def _():
            for q in range(PER):
                chunk = p * PER + q
                remote(chunk_of(early, 0, chunk), chunk_of(early, 2, chunk), own_send.at[2], e2_recv.at[chunk], up).start()
            remote(piece, piece_of(early, 3, p), own_send.at[3], one_recv.at[0], down).start()

            @pl.when(is_a)
            def _():
                remote(piece, piece_of(early, 4, p), own_send.at[4], one_recv.at[1], beside).start()

        @pl.when(hub_f == 0)
        def _():
            remote(piece, piece_of(early, 1, p), own_send.at[2], e1_recv.at[p], beside).start()

        remote(piece, piece_of(late_a, x_from, p), own_send.at[0], late_recv.at[x_from, p], x_up).start()
        remote(piece, piece_of(late_b, x_from, p), own_send.at[1], late_recv.at[2 + x_from, p], x_down).start()

        @pl.when(hub)
        def _():
            remote(piece, piece_of(early, 1, p), own_send.at[5], one_recv.at[2], mate).start()

    send_own(0)

    def rest(p, carry):
        normalize(p)
        send_own(p)
        return carry

    lax.fori_loop(1, PIECES, rest, 0)

    @pl.when(hub)
    def _():
        arrived(meta_e.at[1], meta_recv.at[1])
        meta_copy(meta_e.at[1], meta_l.at[0], LATE, 6, up).start()
        meta_copy(meta_e.at[1], meta_l.at[1], LATE + 1, 7, down).start()

        @pl.when(is_a)
        def _():
            meta_copy(meta_e.at[1], meta_l.at[2], LATE + 2, 8, beside).start()

        arrived(meta_e.at[2], meta_recv.at[2])

        @pl.when(is_b)
        def _():
            meta_copy(meta_e.at[2], meta_e.at[4], 4, 5, beside).start()

        def take(p, carry):
            for q in range(PER):
                chunk = p * PER + q
                src = chunk_of(early, 2, chunk)
                arrived(src, e2_recv.at[chunk])

                @pl.when(is_b)
                def _(src=src, chunk=chunk):
                    remote(src, chunk_of(early, 4, chunk), own_send.at[4], one_recv.at[1], beside).start()

            piece = piece_of(early, 1, p)
            arrived(piece, e1_recv.at[p])
            for q in range(PER):
                chunk = p * PER + q
                remote(chunk_of(early, 1, chunk), chunk_of(late_a, 0, chunk), fwd_send.at[0], l0_recv.at[chunk], up).start()
            remote(piece, piece_of(late_a, 1, p), fwd_send.at[1], late_recv.at[1, p], down).start()

            @pl.when(is_a)
            def _():
                remote(piece, piece_of(late_b, 0, p), fwd_send.at[2], late_recv.at[2, p], beside).start()
            return carry

        lax.fori_loop(0, PIECES, take, 0)
        arrived(meta_l.at[0], meta_recv.at[LATE])

        @pl.when(is_b)
        def _():
            meta_copy(meta_l.at[0], meta_l.at[2], LATE + 2, 8, beside).start()

        arrived(early.at[3], one_recv.at[0])
        arrived(early.at[4], one_recv.at[1])
        for item in (3, 4):
            arrived(meta_e.at[item], meta_recv.at[item])
        for item in (1, 2):
            arrived(meta_l.at[item], meta_recv.at[LATE + item])

    @pl.when(hub_f == 0)
    def _():
        arrived(early.at[1], one_recv.at[2])
        arrived(meta_e.at[1], meta_recv.at[1])
        for item in range(4):
            arrived(meta_l.at[item], meta_recv.at[LATE + item])

    copies = [pltpu.make_async_copy(meta_e.at[item, BLOCKS], tabs.at[item], tab_sem.at[item]) for item in range(5)]
    copies += [pltpu.make_async_copy(meta_l.at[item, BLOCKS], tabs.at[LATE + item], tab_sem.at[LATE + item])
               for item in range(4)]
    for copy in copies:
        copy.start()
    for copy in copies:
        copy.wait()

    best[...] = jnp.full(best.shape, FILL, jnp.float32)

    def by_role(for_hub, for_clus):
        return for_clus + (for_hub - for_clus) * hub_f

    def lists(for_hub, for_clus):
        fields = []
        for f in range(2):
            ours, theirs = packed([e[f] for e in for_hub], 3), packed([e[f] for e in for_clus], 3)
            fields.append([by_role(ours[w], theirs[w]) for w in range(2)])
        return fields + [by_role(flags([e[2] == 1 for e in for_hub]), flags([e[2] == 1 for e in for_clus]))]

    todo = (lists(EE_HUB, EE_CLUS), lists(EL_HUB, EL_CLUS), lists(LL_HUB, LL_CLUS))
    offsets = []
    for f in range(2):
        a, b, c_ = (packed([p[f] for p in place], 2)[0] for place in (PLACE_A, PLACE_B, PLACE_C))
        offsets.append(by_role(a + (b - a) * (yy % 2), c_))

    line = lax.broadcasted_iota(jnp.int32, (16, 128), 0)
    block_at = line // 4

    def look_up(kind, at):
        second_word = at // WORD
        shift = 3 * (at - WORD * second_word)
        row, col = (((words[0] + (words[1] - words[0]) * second_word) >> shift) & 7 for words in todo[kind][:2])
        asks = (todo[kind][2] >> at) & 1
        row_item = row + (LATE if kind == 2 else 0)
        col_item = col + (LATE if kind > 0 else 0)
        asker = row_item + (col_item - row_item) * asks
        other = row_item + col_item - asker
        first, second = ((offset >> (2 * other)) & 3 for offset in offsets)
        place_c = ((x + first) % 4) * 2 + (k + second) % 2
        place_g = 8 + ((z + first) % 4) * 4 + (y + second) % 4
        in_grp = hub_f
        if kind == 0:
            own_pair = 1 - jnp.minimum(at // 2, 1)
            in_grp = own_pair * at + (1 - own_pair) * hub_f
        place = in_grp * place_g + (1 - in_grp) * place_c
        return row, col, row_item, col_item, tabs[asker, asks, place], tabs[asker, 1 - asks, place], tabs[asker, 2, place]

    def labels_down(meta, item, block):
        labs = [meta[item, block, i:i + 1, :].astype(jnp.float32) for i in range(4)]
        return [jnp.transpose(jnp.broadcast_to(lab, (128, 128))) for lab in labs]

    def raise_best(item, values, where):
        best[item] = jnp.maximum(best[item], jnp.where(where, values, FILL))

    def full(scalar):
        return jnp.full((16, 128), scalar, jnp.int32)

    def score(rows, cols, row_labs, col_labs, off, row_best, col_best):
        cosine = lax.dot_general(rows, cols, (((1,), (1,)), ((), ())), preferred_element_type=jnp.float32)
        for j, col_lab in enumerate(col_labs):
            line_best = None
            for i in range(4):
                tile = cosine[i * 128:(i + 1) * 128, j * 128:(j + 1) * 128]
                keep = row_labs[i] == col_lab
                if off is not None and i == len(col_best):
                    keep = keep & off
                tile = jnp.where(keep, tile, FILL)
                row_best[i] = tile if row_best[i] is None else jnp.maximum(row_best[i], tile)
                folded = jnp.max(tile.reshape(16, 8, 128), axis=0)
                line_best = folded if line_best is None else jnp.maximum(line_best, folded)
            col_best.append(jnp.max(line_best, axis=0, keepdims=True))

    def down_rows(row_best):
        return jnp.concatenate([jnp.max(jnp.transpose(t), axis=0, keepdims=True) for t in row_best] * 4, axis=0)

    def pair(kind, at):
        row, col, row_item, col_item, row_block, col_block, alive = look_up(kind, at)
        row_ref, row_meta = (late_a, meta_l) if kind == 2 else (early, meta_e)
        col_ref, col_meta = (late_a if at == 0 else late_b, meta_l) if kind == 2 else (early, meta_e)
        col_at = col - 2 if kind == 2 and at > 0 else col
        rows = row_ref[row, row_block]
        row_labs = labels_down(row_meta, row, row_block)
        col_labs = [col_meta[col, col_block, i:i + 1, :].astype(jnp.float32) for i in range(4)]
        off = None
        if kind == 0:
            apart = jnp.where((row == col) & (row_block == col_block), 0, 1)
            off = (lax.broadcasted_iota(jnp.int32, (128, 128), 0) != lax.broadcasted_iota(jnp.int32, (128, 128), 1))
            off = off | (jnp.full((128, 128), apart, jnp.int32) > 0)
        row_best, col_best = [None] * 4, []
        for n in range(2):
            cols = col_ref[col_at, col_block, n * PIECE:(n + 1) * PIECE, :]
            score(rows, cols, row_labs, col_labs[2 * n:2 * n + 2], off, row_best, col_best)
        raise_best(row_item, down_rows(row_best), (block_at == row_block) & (full(alive) > 0))
        raise_best(col_item, jnp.concatenate(col_best * 4, axis=0), (block_at == col_block) & (full(alive) > 0))

    def late_pair(at, p):
        row, col, row_item, col_item, row_block, col_block, alive = look_up(1, at)
        block, half = p // 2, p % 2
        rows = early[row, row_block]
        row_labs = labels_down(meta_e, row, row_block)
        col_labs = [meta_l[col, block, pl.ds(half * 2 + j, 1), :].astype(jnp.float32) for j in range(2)]
        row_best, col_best = [None] * 4, []
        cols = piece_of(late_a, col, p) if at < EL_A else piece_of(late_b, col - 2, p)
        score(rows, cols[...], row_labs, col_labs, None, row_best, col_best)
        asked = full(jnp.where(col_block == block, alive, 0)) > 0
        raise_best(row_item, down_rows(row_best), (block_at == row_block) & asked)
        at_line = block * 4 + half * 2
        both = jnp.where(line == at_line, col_best[0], col_best[1])
        raise_best(col_item, both, asked & ((line == at_line) | (line == at_line + 1)))

    def pass_on(p, q):
        chunk = p * PER + q

        @pl.when(hub & (p < PIECES))
        def _():
            src = chunk_of(late_a, 0, chunk)
            arrived(src, l0_recv.at[chunk])

            @pl.when(is_b)
            def _():
                remote(src, chunk_of(late_b, 0, chunk), fwd_send.at[2], late_recv.at[2, p], beside).start()

    early_pairs = len(EE_CLUS) + (len(EE_HUB) - 2 - len(EE_CLUS)) * hub_f

    def step(p, carry):
        pass_on(p, 0)

        @pl.when(2 * p < early_pairs)
        def _():
            pair(0, 2 * p)
            pair(0, 2 * p + 1)

        pass_on(p, 1)

        @pl.when(p > 0)
        def _():
            arrived(piece_of(late_a, 1, p - 1), late_recv.at[1, p - 1])

            @pl.when(hub_f == 0)
            def _():
                arrived(piece_of(late_a, 0, p - 1), late_recv.at[0, p - 1])

            for at in range(EL_A):
                late_pair(at, p - 1)

        pass_on(p, 2)

        @pl.when(hub & (p == PIECES))
        def _():
            pair(2, 0)

        @pl.when(p > 0)
        def _():
            arrived(piece_of(late_b, 0, p - 1), late_recv.at[2, p - 1])

            @pl.when(hub_f == 0)
            def _():
                arrived(piece_of(late_b, 1, p - 1), late_recv.at[3, p - 1])

            for at in range(EL_A, len(EL_HUB)):
                late_pair(at, p - 1)

        pass_on(p, 3)
        return carry

    @pl.when(hub)
    def _():
        pair(0, 16)
        pair(0, 17)

    lax.fori_loop(0, PIECES + 1, step, 0)
    pair(2, 1)
    pair(2, 2)

    @pl.when(hub_f == 0)
    def _():
        pair(2, 3)
        pair(2, 4)

    def give(item, to, send, device):
        return remote(best.at[item], ret.at[to], ret_send.at[send], ret_recv.at[to], device)

    def hub_gives(a):
        return [give(1, 0, 0, dev(0, k, 0, 3 if a else 1)), give(2, 0, 1, dev(0, k, 3, 0)), give(3, 1, 2, dev(0, k, 1, 0)),
                give(4, 2, 3, dev(0, k, 3, 1) if a else dev(0, k, 0, 3)),
                give(5, 1, 4, dev(0, k, 3, 3 if a else 1)), give(6, 2, 5, dev(0, k, 1, 3 if a else 1)),
                give(7, 3, 6, dev(0, k, 3, 2) if a else dev(0, k, 0, 2))]

    def clus_gives():
        return [give(1, 3, 0, mate), give(5, 4, 1, dev(3, 1 - k, 0, 0)), give(6, 4, 2, dev(3, k, 0, 0)),
                give(7, 5, 3, dev(1, 1 - k, 0, 0)), give(8, 5, 4, dev(1, k, 0, 0))]

    for which, gives in ((is_a, lambda: hub_gives(True)), (is_b, lambda: hub_gives(False)), (hub_f == 0, clus_gives)):
        @pl.when(which)
        def _(gives=gives):
            for copy in gives():
                copy.start()

    for s in range(2):
        arrived(early.at[0], own_send.at[s])
        arrived(meta_e.at[0], meta_send.at[s])

    @pl.when(hub)
    def _():
        for s in range(2, 6):
            arrived(early.at[0], own_send.at[s])
        for s in range(3):
            arrived(early.at[0], fwd_send.at[s])
        for s in range(2, 9):
            arrived(meta_e.at[0], meta_send.at[s])
        for s in range(7):
            arrived(best.at[0], ret_send.at[s])

    @pl.when(hub_f == 0)
    def _():
        arrived(early.at[0], own_send.at[2])
        arrived(meta_e.at[0], meta_send.at[2])
        for s in range(5):
            arrived(best.at[0], ret_send.at[s])

    result = best[0]
    for j in range(6):
        arrived(ret.at[j], ret_recv.at[j])
        result = jnp.maximum(result, ret[j])
    out[...] = result


def on_device(embeddings, labels, partner_block, own_block, live):
    dma = pltpu.SemaphoreType.DMA
    vmem = pl.BlockSpec(memory_space=pltpu.VMEM)
    best = pl.pallas_call(
        kernel,
        out_shape=jax.ShapeDtypeStruct((16, 128), jnp.float32),
        in_specs=[pl.BlockSpec(memory_space=pl.ANY), vmem, vmem, vmem, vmem],
        out_specs=vmem,
        scratch_shapes=[
            pltpu.VMEM((5, BLOCKS, BLOCK, D), jnp.bfloat16),
            pltpu.VMEM((2, BLOCKS, BLOCK, D), jnp.bfloat16),
            pltpu.VMEM((2, BLOCKS, BLOCK, D), jnp.bfloat16),
            pltpu.VMEM((5, BLOCKS + 1, 8, 128), jnp.int32),
            pltpu.VMEM((4, BLOCKS + 1, 8, 128), jnp.int32),
            pltpu.SMEM((9, 8, 128), jnp.int32),
            pltpu.VMEM((9, 16, 128), jnp.float32),
            pltpu.VMEM((6, 16, 128), jnp.float32),
            dma((PIECES,)), dma((9,)), dma((6,)), dma((3,)), dma((9,)), dma((7,)),
            dma((PIECES,)), dma((CHUNKS,)), dma((CHUNKS,)), dma((4, PIECES)), dma((3,)), dma((9,)), dma((6,)),
        ],
        compiler_params=pltpu.CompilerParams(collective_id=0, has_side_effects=True, vmem_limit_bytes=56 << 20),
        cost_estimate=pl.CostEstimate(flops=24 * 2 * 512 * 512 * 1024, bytes_accessed=4 << 20, transcendentals=2048),
    )(embeddings, labels.reshape(16, 128), own_block, partner_block, live)
    return best.reshape(2048)


def solution(mesh):
    placed = (
        P(("clus", "grp"), None),
        P(("clus", "grp")),
        P(("clus", "grp"), None),
        P(("clus", "grp"), None),
        P(("clus", "grp"), None),
    )
    return jax.shard_map(
        on_device, mesh=mesh, in_specs=placed, out_specs=P(("clus", "grp")), check_vma=False
    )
```

```python
import jax
import jax.numpy as jnp
from jax import lax
from jax.experimental import pallas as pl
from jax.experimental.pallas import tpu as pltpu
from jax.sharding import PartitionSpec as P

MESH = pl.DeviceIdType.MESH
ROWS = 2048
D = 1024
BLOCK = 512
BLOCKS = ROWS // BLOCK
EPS = 1e-06
FILL = -1.0

PIECE = 256
PIECES = ROWS // PIECE
CHUNK = 64
CHUNKS = ROWS // CHUNK
PER = PIECE // CHUNK

EE_HUB = [(0, 0, 0), (0, 0, 0), (0, 1, 0), (0, 1, 1), (0, 2, 0), (0, 3, 0), (2, 3, 0), (1, 2, 0), (1, 2, 1),
          (1, 3, 0), (1, 3, 1), (0, 4, 0), (0, 4, 1), (1, 4, 0), (1, 4, 1), (3, 4, 0), (3, 4, 1), (3, 4, 1)]
EL_HUB = [(1, 0, 0), (1, 1, 0), (2, 1, 0), (2, 1, 1), (4, 1, 0), (4, 1, 1), (3, 2, 0), (3, 2, 1),
          (0, 2, 0), (0, 2, 1), (1, 2, 0), (1, 2, 1)]
LL_HUB = [(0, 1, 0), (1, 2, 0), (1, 2, 1), (1, 2, 1), (1, 2, 1)]
EE_CLUS = [(0, 0, 0), (0, 0, 0), (0, 1, 0), (0, 1, 1)]
EL_CLUS = [(0, 1, 0), (0, 1, 1), (1, 0, 0), (1, 0, 1), (0, 1, 0), (0, 1, 1),
           (0, 2, 0), (0, 2, 1), (1, 3, 0), (1, 3, 1), (0, 2, 0), (0, 2, 1)]
LL_CLUS = [(0, 1, 0), (0, 2, 0), (0, 3, 0), (1, 2, 0), (1, 3, 0)]
EL_A = 6
PLACE_A = [(0, 0), (0, 3), (3, 0), (1, 0), (3, 1), (3, 3), (1, 3), (3, 2), (0, 0)]
PLACE_B = [(0, 0), (0, 1), (3, 0), (1, 0), (0, 3), (3, 1), (1, 1), (0, 2), (0, 0)]
PLACE_C = [(0, 0), (0, 1), (0, 0), (0, 0), (0, 0), (3, 1), (3, 0), (1, 1), (1, 0)]
LATE = 5
WORD = 9


def packed(values, bits):
    words = [0, 0]
    for at, value in enumerate(values):
        words[at // WORD] |= value << bits * (at % WORD)
    return words


def flags(values):
    return sum(int(value) << at for at, value in enumerate(values))


def kernel(emb, labs_in, own_in, part_in, live_in, out, early, late_a, late_b, labs, small, meta_e, meta_l, tabs, best, ret,
           in_sem, tab_sem, own_send, fwd_send, meta_send, ret_send,
           e1_recv, e2_recv, l0_recv, late_recv, one_recv, meta_recv, ret_recv):
    c = lax.axis_index("clus")
    g = lax.axis_index("grp")
    x, k = c // 2, c % 2
    z, y = g // 4, g % 4
    yy = (y + 2 * k) % 4
    hub = yy < 2
    hub_f = 1 - yy // 2
    is_a, is_b = yy == 0, yy == 1
    kc = 1 - y // 2

    def dev(dx, core, dz, dy):
        return (((x + dx) % 4) * 2 + core, ((z + dz) % 4) * 4 + (y + dy) % 4)

    up, down = dev(0, k, 1, 0), dev(0, k, 3, 0)
    mate = dev(0, 1 - k, 0, 0)
    x_up, x_down = dev(1, kc, 0, 0), dev(3, kc, 0, 0)
    beside = dev(0, k, 0, 1 + 2 * ((yy + 1) // 2 % 2))

    barrier = pltpu.get_barrier_semaphore()

    def greet(*devices):
        for device in devices:
            pl.semaphore_signal(barrier, inc=1, device_id=device, device_id_type=MESH)

    @pl.when(hub)
    def _():
        greet(up, down, beside, dev(0, k, 0, 3 - 2 * (yy % 2)))

    @pl.when(hub_f == 0)
    def _():
        greet(mate, x_up, x_down, dev(1, 1 - k, 0, 0), dev(3, 1 - k, 0, 0))

    def part_of(ref, item, at, size):
        per = BLOCK // size
        return ref.at[item, at // per, pl.ds(pl.multiple_of(at % per * size, size), size)]

    def piece_of(ref, item, p):
        return part_of(ref, item, p, PIECE)

    def chunk_of(ref, item, chunk):
        return part_of(ref, item, chunk, CHUNK)

    def piece_in(p):
        return pltpu.make_async_copy(emb.at[pl.ds(p * PIECE, PIECE)], piece_of(early, 0, p), in_sem.at[p])

    into = [pltpu.make_async_copy(labs_in, labs, in_sem.at[PIECES])]
    into += [pltpu.make_async_copy(tab, small.at[at], in_sem.at[PIECES + 1 + at])
             for at, tab in enumerate((own_in, part_in, live_in))]
    piece_in(0).start()
    for copy in into:
        copy.start()
    for p in range(1, PIECES):
        piece_in(p).start()
    for copy in into:
        copy.wait()
    for b in range(BLOCKS):
        meta_e[0, b, 0:4, :] = labs[4 * b:4 * b + 4, :]
    for at in range(3):
        meta_e[0, BLOCKS, at:at + 1, 0:24] = small[at]

    def remote(src, dst, send, recv, device):
        return pltpu.make_async_remote_copy(src_ref=src, dst_ref=dst, send_sem=send, recv_sem=recv,
                                            device_id=device, device_id_type=MESH)

    def arrived(ref, sem):
        pltpu.make_async_copy(ref, ref, sem).wait()

    def meta_copy(src, dst, item, send, device):
        return remote(src, dst, meta_send.at[send], meta_recv.at[item], device)

    def normalize(p):
        piece_in(p).wait()
        rows = piece_of(early, 0, p)
        wide = rows[...].astype(jnp.float32)
        inverse = lax.rsqrt(jnp.sum(wide * wide, axis=1, keepdims=True) + EPS)
        rows[...] = (wide * inverse).astype(jnp.bfloat16)

    best[...] = jnp.full(best.shape, FILL, jnp.float32)
    normalize(0)
    pl.semaphore_wait(barrier, 3 + 3 * hub_f)

    x_from = 1 - hub_f
    def send_own(p):
        piece = piece_of(early, 0, p)

        @pl.when(hub)
        def _():
            for q in range(PER):
                chunk = p * PER + q
                remote(chunk_of(early, 0, chunk), chunk_of(early, 2, chunk), own_send.at[2], e2_recv.at[chunk], up).start()
            remote(piece, piece_of(early, 3, p), own_send.at[3], one_recv.at[0], down).start()

            @pl.when(is_a)
            def _():
                remote(piece, piece_of(early, 4, p), own_send.at[4], one_recv.at[1], beside).start()

        @pl.when(hub_f == 0)
        def _():
            remote(piece, piece_of(early, 1, p), own_send.at[2], e1_recv.at[p], beside).start()

        remote(piece, piece_of(late_a, x_from, p), own_send.at[0], late_recv.at[x_from, p], x_up).start()
        remote(piece, piece_of(late_b, x_from, p), own_send.at[1], late_recv.at[2 + x_from, p], x_down).start()

        @pl.when(hub)
        def _():
            remote(piece, piece_of(early, 1, p), own_send.at[5], one_recv.at[2], mate).start()

    def across_early(chunk):
        src = chunk_of(early, 2, chunk)
        arrived(src, e2_recv.at[chunk])

        @pl.when(is_b)
        def _():
            remote(src, chunk_of(early, 4, chunk), own_send.at[4], one_recv.at[1], beside).start()

    meta_copy(meta_e.at[0], meta_l.at[x_from], LATE + x_from, 0, x_up).start()
    meta_copy(meta_e.at[0], meta_l.at[2 + x_from], LATE + 2 + x_from, 1, x_down).start()

    @pl.when(hub)
    def _():
        meta_copy(meta_e.at[0], meta_e.at[2], 2, 2, up).start()
        meta_copy(meta_e.at[0], meta_e.at[3], 3, 3, down).start()
        meta_copy(meta_e.at[0], meta_e.at[1], 1, 4, mate).start()

        @pl.when(is_a)
        def _():
            meta_copy(meta_e.at[0], meta_e.at[4], 4, 5, beside).start()

    @pl.when(hub_f == 0)
    def _():
        meta_copy(meta_e.at[0], meta_e.at[1], 1, 2, beside).start()

    send_own(0)

    def rest(p, carry):
        normalize(p)
        send_own(p)

        @pl.when(hub & (p >= PIECES - PER))
        def _():
            across_early(p - (PIECES - PER))
        return carry

    lax.fori_loop(1, PIECES, rest, 0)

    copies = [pltpu.make_async_copy(meta_e.at[item, BLOCKS], tabs.at[item], tab_sem.at[item]) for item in range(5)]
    copies += [pltpu.make_async_copy(meta_l.at[item, BLOCKS], tabs.at[LATE + item], tab_sem.at[LATE + item])
               for item in range(4)]

    @pl.when(hub)
    def _():
        arrived(meta_e.at[1], meta_recv.at[1])
        meta_copy(meta_e.at[1], meta_l.at[0], LATE, 6, up).start()
        meta_copy(meta_e.at[1], meta_l.at[1], LATE + 1, 7, down).start()

        @pl.when(is_a)
        def _():
            meta_copy(meta_e.at[1], meta_l.at[2], LATE + 2, 8, beside).start()

        arrived(meta_e.at[2], meta_recv.at[2])

        @pl.when(is_b)
        def _():
            meta_copy(meta_e.at[2], meta_e.at[4], 4, 5, beside).start()

        def take(p, carry):
            @pl.when(p < PIECES - 1)
            def _():
                for q in range(PER):
                    across_early((p + 1) * PER + q)

            piece = piece_of(early, 1, p)
            arrived(piece, e1_recv.at[p])
            for q in range(PER):
                chunk = p * PER + q
                remote(chunk_of(early, 1, chunk), chunk_of(late_a, 0, chunk), fwd_send.at[0], l0_recv.at[chunk], up).start()
            remote(piece, piece_of(late_a, 1, p), fwd_send.at[1], late_recv.at[1, p], down).start()

            @pl.when(is_a)
            def _():
                remote(piece, piece_of(late_b, 0, p), fwd_send.at[2], late_recv.at[2, p], beside).start()
            return carry

        lax.fori_loop(0, PIECES, take, 0)
        arrived(meta_l.at[0], meta_recv.at[LATE])

        @pl.when(is_b)
        def _():
            meta_copy(meta_l.at[0], meta_l.at[2], LATE + 2, 8, beside).start()

    @pl.when(hub_f == 0)
    def _():
        arrived(early.at[1], one_recv.at[2])
        arrived(meta_e.at[1], meta_recv.at[1])
        for item in range(4):
            arrived(meta_l.at[item], meta_recv.at[LATE + item])
        for copy in copies:
            copy.start()
        for copy in copies:
            copy.wait()

    def by_role(for_hub, for_clus):
        return for_clus + (for_hub - for_clus) * hub_f

    def lists(for_hub, for_clus):
        fields = []
        for f in range(2):
            ours, theirs = packed([e[f] for e in for_hub], 3), packed([e[f] for e in for_clus], 3)
            fields.append([by_role(ours[w], theirs[w]) for w in range(2)])
        return fields + [by_role(flags([e[2] == 1 for e in for_hub]), flags([e[2] == 1 for e in for_clus]))]

    todo = (lists(EE_HUB, EE_CLUS), lists(EL_HUB, EL_CLUS), lists(LL_HUB, LL_CLUS))
    offsets = []
    for f in range(2):
        a, b, c_ = (packed([p[f] for p in place], 2)[0] for place in (PLACE_A, PLACE_B, PLACE_C))
        offsets.append(by_role(a + (b - a) * (yy % 2), c_))

    line = lax.broadcasted_iota(jnp.int32, (16, 128), 0)
    block_at = line // 4

    def look_up(kind, at):
        second_word = at // WORD
        shift = 3 * (at - WORD * second_word)
        row, col = (((words[0] + (words[1] - words[0]) * second_word) >> shift) & 7 for words in todo[kind][:2])
        asks = (todo[kind][2] >> at) & 1
        row_item = row + (LATE if kind == 2 else 0)
        col_item = col + (LATE if kind > 0 else 0)
        asker = row_item + (col_item - row_item) * asks
        other = row_item + col_item - asker
        first, second = ((offset >> (2 * other)) & 3 for offset in offsets)
        place_c = ((x + first) % 4) * 2 + (k + second) % 2
        place_g = 8 + ((z + first) % 4) * 4 + (y + second) % 4
        in_grp = hub_f
        if kind == 0:
            own_pair = 1 - jnp.minimum(at // 2, 1)
            in_grp = own_pair * at + (1 - own_pair) * hub_f
        place = in_grp * place_g + (1 - in_grp) * place_c
        return row, col, row_item, col_item, tabs[asker, asks, place], tabs[asker, 1 - asks, place], tabs[asker, 2, place]

    def labels_down(meta, item, block):
        labs = [meta[item, block, i:i + 1, :].astype(jnp.float32) for i in range(4)]
        return [jnp.transpose(jnp.broadcast_to(lab, (128, 128))) for lab in labs]

    def raise_best(item, values, where):
        best[item] = jnp.maximum(best[item], jnp.where(where, values, FILL))

    def full(scalar):
        return jnp.full((16, 128), scalar, jnp.int32)

    def score(rows, cols, row_labs, col_labs, off, row_best, col_best):
        cosine = lax.dot_general(rows, cols, (((1,), (1,)), ((), ())), preferred_element_type=jnp.float32)
        for j, col_lab in enumerate(col_labs):
            line_best = None
            for i in range(4):
                tile = cosine[i * 128:(i + 1) * 128, j * 128:(j + 1) * 128]
                keep = row_labs[i] == col_lab
                if off is not None and i == len(col_best):
                    keep = keep & off
                tile = jnp.where(keep, tile, FILL)
                row_best[i] = tile if row_best[i] is None else jnp.maximum(row_best[i], tile)
                folded = jnp.max(tile.reshape(16, 8, 128), axis=0)
                line_best = folded if line_best is None else jnp.maximum(line_best, folded)
            col_best.append(jnp.max(line_best, axis=0, keepdims=True))

    def down_rows(row_best):
        return jnp.concatenate([jnp.max(jnp.transpose(t), axis=0, keepdims=True) for t in row_best] * 4, axis=0)

    def pair(kind, at):
        row, col, row_item, col_item, row_block, col_block, alive = look_up(kind, at)
        row_ref, row_meta = (late_a, meta_l) if kind == 2 else (early, meta_e)
        col_ref, col_meta = (late_a if at == 0 else late_b, meta_l) if kind == 2 else (early, meta_e)
        col_at = col - 2 if kind == 2 and at > 0 else col
        rows = row_ref[row, row_block]
        row_labs = labels_down(row_meta, row, row_block)
        col_labs = [col_meta[col, col_block, i:i + 1, :].astype(jnp.float32) for i in range(4)]
        off = None
        if kind == 0:
            apart = jnp.where((row == col) & (row_block == col_block), 0, 1)
            off = (lax.broadcasted_iota(jnp.int32, (128, 128), 0) != lax.broadcasted_iota(jnp.int32, (128, 128), 1))
            off = off | (jnp.full((128, 128), apart, jnp.int32) > 0)
        row_best, col_best = [None] * 4, []
        for n in range(2):
            cols = col_ref[col_at, col_block, n * PIECE:(n + 1) * PIECE, :]
            score(rows, cols, row_labs, col_labs[2 * n:2 * n + 2], off, row_best, col_best)
        raise_best(row_item, down_rows(row_best), (block_at == row_block) & (full(alive) > 0))
        raise_best(col_item, jnp.concatenate(col_best * 4, axis=0), (block_at == col_block) & (full(alive) > 0))

    def late_pair(at, p):
        row, col, row_item, col_item, row_block, col_block, alive = look_up(1, at)
        block, half = p // 2, p % 2
        rows = early[row, row_block]
        row_labs = labels_down(meta_e, row, row_block)
        col_labs = [meta_l[col, block, pl.ds(half * 2 + j, 1), :].astype(jnp.float32) for j in range(2)]
        row_best, col_best = [None] * 4, []
        cols = piece_of(late_a, col, p) if at < EL_A else piece_of(late_b, col - 2, p)
        score(rows, cols[...], row_labs, col_labs, None, row_best, col_best)
        asked = full(jnp.where(col_block == block, alive, 0)) > 0
        raise_best(row_item, down_rows(row_best), (block_at == row_block) & asked)
        at_line = block * 4 + half * 2
        both = jnp.where(line == at_line, col_best[0], col_best[1])
        raise_best(col_item, both, asked & ((line == at_line) | (line == at_line + 1)))

    def pass_on(p, q):
        chunk = p * PER + q

        @pl.when(hub)
        def _():
            src = chunk_of(late_a, 0, chunk)
            arrived(src, l0_recv.at[chunk])

            @pl.when(is_b)
            def _():
                remote(src, chunk_of(late_b, 0, chunk), fwd_send.at[2], late_recv.at[2, p], beside).start()

    early_pairs = len(EE_CLUS) + (len(EE_HUB) - 2 - len(EE_CLUS)) * hub_f

    def late_a_pairs(p):
        arrived(piece_of(late_a, 1, p), late_recv.at[1, p])

        @pl.when(hub_f == 0)
        def _():
            arrived(piece_of(late_a, 0, p), late_recv.at[0, p])

        for at in range(EL_A):
            late_pair(at, p)

    def late_b_pairs(p):
        arrived(piece_of(late_b, 0, p), late_recv.at[2, p])

        @pl.when(hub_f == 0)
        def _():
            arrived(piece_of(late_b, 1, p), late_recv.at[3, p])

        for at in range(EL_A, len(EL_HUB)):
            late_pair(at, p)

    def step(p, carry):
        pass_on(p, 0)

        @pl.when(hub & (p == 0))
        def _():
            arrived(early.at[3], one_recv.at[0])
            arrived(early.at[4], one_recv.at[1])
            for item in (3, 4):
                arrived(meta_e.at[item], meta_recv.at[item])
            for item in (1, 2):
                arrived(meta_l.at[item], meta_recv.at[LATE + item])
            for copy in copies:
                copy.start()
            for copy in copies:
                copy.wait()

        @pl.when(2 * p < early_pairs)
        def _():
            pair(0, 2 * p)
            pair(0, 2 * p + 1)

        pass_on(p, 1)

        @pl.when(p > 0)
        def _():
            late_a_pairs(p - 1)

        @pl.when(hub & (p == 0))
        def _():
            pair(0, 16)
            pair(0, 17)

        pass_on(p, 2)

        @pl.when(p > 0)
        def _():
            late_b_pairs(p - 1)

        pass_on(p, 3)
        return carry

    lax.fori_loop(0, PIECES, step, 0)
    late_a_pairs(PIECES - 1)
    late_b_pairs(PIECES - 1)
    for at in range(3):
        pair(2, at)

    @pl.when(hub_f == 0)
    def _():
        pair(2, 3)
        pair(2, 4)

    def give(item, to, send, device):
        return remote(best.at[item], ret.at[to], ret_send.at[send], ret_recv.at[to], device)

    def hub_gives(a):
        return [give(1, 0, 0, dev(0, k, 0, 3 if a else 1)), give(2, 0, 1, dev(0, k, 3, 0)), give(3, 1, 2, dev(0, k, 1, 0)),
                give(4, 2, 3, dev(0, k, 3, 1) if a else dev(0, k, 0, 3)),
                give(5, 1, 4, dev(0, k, 3, 3 if a else 1)), give(6, 2, 5, dev(0, k, 1, 3 if a else 1)),
                give(7, 3, 6, dev(0, k, 3, 2) if a else dev(0, k, 0, 2))]

    def clus_gives():
        return [give(1, 3, 0, mate), give(5, 4, 1, dev(3, 1 - k, 0, 0)), give(6, 4, 2, dev(3, k, 0, 0)),
                give(7, 5, 3, dev(1, 1 - k, 0, 0)), give(8, 5, 4, dev(1, k, 0, 0))]

    for which, gives in ((is_a, lambda: hub_gives(True)), (is_b, lambda: hub_gives(False)), (hub_f == 0, clus_gives)):
        @pl.when(which)
        def _(gives=gives):
            for copy in reversed(gives()):
                copy.start()

    for s in range(2):
        arrived(early.at[0], own_send.at[s])
        arrived(meta_e.at[0], meta_send.at[s])

    @pl.when(hub)
    def _():
        for s in range(2, 6):
            arrived(early.at[0], own_send.at[s])
        for s in range(3):
            arrived(early.at[0], fwd_send.at[s])
        for s in range(2, 9):
            arrived(meta_e.at[0], meta_send.at[s])
        for s in range(7):
            arrived(best.at[0], ret_send.at[s])

    @pl.when(hub_f == 0)
    def _():
        arrived(early.at[0], own_send.at[2])
        arrived(meta_e.at[0], meta_send.at[2])
        for s in range(5):
            arrived(best.at[0], ret_send.at[s])

    result = best[0]
    for j in range(6):
        arrived(ret.at[j], ret_recv.at[j])
        result = jnp.maximum(result, ret[j])
    out[...] = result


def on_device(embeddings, labels, partner_block, own_block, live):
    dma = pltpu.SemaphoreType.DMA
    vmem = pl.BlockSpec(memory_space=pltpu.VMEM)
    best = pl.pallas_call(
        kernel,
        out_shape=jax.ShapeDtypeStruct((16, 128), jnp.float32),
        in_specs=[pl.BlockSpec(memory_space=pl.ANY)] * 5,
        out_specs=vmem,
        scratch_shapes=[
            pltpu.VMEM((5, BLOCKS, BLOCK, D), jnp.bfloat16),
            pltpu.VMEM((2, BLOCKS, BLOCK, D), jnp.bfloat16),
            pltpu.VMEM((2, BLOCKS, BLOCK, D), jnp.bfloat16),
            pltpu.VMEM((16, 128), jnp.int32),
            pltpu.VMEM((3, 1, 24), jnp.int32),
            pltpu.VMEM((5, BLOCKS + 1, 8, 128), jnp.int32),
            pltpu.VMEM((4, BLOCKS + 1, 8, 128), jnp.int32),
            pltpu.SMEM((9, 8, 128), jnp.int32),
            pltpu.VMEM((9, 16, 128), jnp.float32),
            pltpu.VMEM((6, 16, 128), jnp.float32),
            dma((PIECES + 4,)), dma((9,)), dma((6,)), dma((3,)), dma((9,)), dma((7,)),
            dma((PIECES,)), dma((CHUNKS,)), dma((CHUNKS,)), dma((4, PIECES)), dma((3,)), dma((9,)), dma((6,)),
        ],
        compiler_params=pltpu.CompilerParams(collective_id=0, has_side_effects=True, vmem_limit_bytes=56 << 20),
        cost_estimate=pl.CostEstimate(flops=24 * 2 * 512 * 512 * 1024, bytes_accessed=4 << 20, transcendentals=2048),
    )(embeddings, labels.reshape(16, 128), own_block, partner_block, live)
    return best.reshape(2048)


def solution(mesh):
    placed = (
        P(("clus", "grp"), None),
        P(("clus", "grp")),
        P(("clus", "grp"), None),
        P(("clus", "grp"), None),
        P(("clus", "grp"), None),
    )
    return jax.shard_map(
        on_device, mesh=mesh, in_specs=placed, out_specs=P(("clus", "grp")), check_vma=False
    )
```

```python
import jax
import jax.numpy as jnp
from jax import lax
from jax.experimental import pallas as pl
from jax.experimental.pallas import tpu as pltpu
from jax.sharding import PartitionSpec as P

MESH = pl.DeviceIdType.MESH
ROWS = 2048
D = 1024
BLOCK = 512
BLOCKS = ROWS // BLOCK
EPS = 1e-06
FILL = -1.0

PIECE = 256
PIECES = ROWS // PIECE
PER = 4
CHUNKS = PIECES * PER
WIDTH = D // PER
HALF = D // 2

EE_HUB = [(0, 0, 0), (0, 0, 0), (0, 1, 0), (0, 1, 1), (0, 2, 0), (0, 3, 0), (2, 3, 0), (1, 2, 0), (1, 2, 1),
          (1, 3, 0), (1, 3, 1), (0, 4, 0), (0, 4, 1), (1, 4, 0), (1, 4, 1), (3, 4, 0), (3, 4, 1), (3, 4, 1)]
EL_HUB = [(1, 0, 0), (1, 1, 0), (2, 1, 0), (2, 1, 1), (4, 1, 0), (4, 1, 1), (3, 2, 0), (3, 2, 1),
          (0, 2, 0), (0, 2, 1), (1, 2, 0), (1, 2, 1)]
LL_HUB = [(0, 1, 0), (1, 2, 0), (1, 2, 1), (1, 2, 1), (1, 2, 1)]
EE_CLUS = [(0, 0, 0), (0, 0, 0), (0, 1, 0), (0, 1, 1)]
EL_CLUS = [(0, 1, 0), (0, 1, 1), (1, 0, 0), (1, 0, 1), (0, 1, 0), (0, 1, 1),
           (0, 2, 0), (0, 2, 1), (1, 3, 0), (1, 3, 1), (0, 2, 0), (0, 2, 1)]
LL_CLUS = [(0, 1, 0), (0, 2, 0), (0, 3, 0), (1, 2, 0), (1, 3, 0)]
EL_A = 6
PLACE_A = [(0, 0), (0, 3), (3, 0), (1, 0), (3, 1), (3, 3), (1, 3), (3, 2), (0, 0)]
PLACE_B = [(0, 0), (0, 1), (3, 0), (1, 0), (0, 3), (3, 1), (1, 1), (0, 2), (0, 0)]
PLACE_C = [(0, 0), (0, 1), (0, 0), (0, 0), (0, 0), (3, 1), (3, 0), (1, 1), (1, 0)]
LATE = 5
WORD = 9


def packed(values, bits):
    words = [0, 0]
    for at, value in enumerate(values):
        words[at // WORD] |= value << bits * (at % WORD)
    return words


def flags(values):
    return sum(int(value) << at for at, value in enumerate(values))


def kernel(emb, labs_in, own_in, part_in, live_in, out, early, late_a, late_b, labs, small, meta_e, meta_l, tabs, best, part, ret,
           in_sem, tab_sem, own_send, fwd_send, meta_send, ret_send,
           e1_recv, e2_recv, l0_recv, late_recv, one_recv, meta_recv, ret_recv):
    c = lax.axis_index("clus")
    g = lax.axis_index("grp")
    x, k = c // 2, c % 2
    z, y = g // 4, g % 4
    yy = (y + 2 * k) % 4
    hub = yy < 2
    hub_f = 1 - yy // 2
    is_a, is_b = yy == 0, yy == 1
    kc = 1 - y // 2

    def dev(dx, core, dz, dy):
        return (((x + dx) % 4) * 2 + core, ((z + dz) % 4) * 4 + (y + dy) % 4)

    up, down = dev(0, k, 1, 0), dev(0, k, 3, 0)
    mate = dev(0, 1 - k, 0, 0)
    x_up, x_down = dev(1, kc, 0, 0), dev(3, kc, 0, 0)
    beside = dev(0, k, 0, 1 + 2 * ((yy + 1) // 2 % 2))

    barrier = pltpu.get_barrier_semaphore()

    def greet(*devices):
        for device in devices:
            pl.semaphore_signal(barrier, inc=1, device_id=device, device_id_type=MESH)

    @pl.when(hub)
    def _():
        greet(up, down, beside, dev(0, k, 0, 3 - 2 * (yy % 2)))

    @pl.when(hub_f == 0)
    def _():
        greet(mate, x_up, x_down, dev(1, 1 - k, 0, 0), dev(3, 1 - k, 0, 0))

    def part_of(ref, item, at, size):
        per = BLOCK // size
        return ref.at[item, at // per, pl.ds(pl.multiple_of(at % per * size, size), size)]

    def piece_of(ref, item, p):
        return part_of(ref, item, p, PIECE)

    def slab_of(ref, item, p, first, width):
        rows = pl.ds(pl.multiple_of(p % 2 * PIECE, PIECE), PIECE)
        return ref.at[item, p // 2, rows, pl.ds(pl.multiple_of(first, width), width)]

    def chunk_of(ref, item, chunk):
        return slab_of(ref, item, chunk // PER, chunk % PER * WIDTH, WIDTH)

    def half_of(ref, item, p, h):
        return slab_of(ref, item, p, h * HALF, HALF)

    def piece_in(p):
        return pltpu.make_async_copy(emb.at[pl.ds(p * PIECE, PIECE)], piece_of(early, 0, p), in_sem.at[p])

    into = [pltpu.make_async_copy(labs_in, labs, in_sem.at[PIECES])]
    into += [pltpu.make_async_copy(tab, small.at[at], in_sem.at[PIECES + 1 + at])
             for at, tab in enumerate((own_in, part_in, live_in))]
    piece_in(0).start()
    for copy in into:
        copy.start()
    for p in range(1, PIECES):
        piece_in(p).start()
    for copy in into:
        copy.wait()
    for b in range(BLOCKS):
        meta_e[0, b, 0:4, :] = labs[4 * b:4 * b + 4, :]
    for at in range(3):
        meta_e[0, BLOCKS, at:at + 1, 0:24] = small[at]

    def remote(src, dst, send, recv, device):
        return pltpu.make_async_remote_copy(src_ref=src, dst_ref=dst, send_sem=send, recv_sem=recv,
                                            device_id=device, device_id_type=MESH)

    def arrived(ref, sem):
        pltpu.make_async_copy(ref, ref, sem).wait()

    def meta_copy(src, dst, item, send, device):
        return remote(src, dst, meta_send.at[send], meta_recv.at[item], device)

    def normalize(p):
        piece_in(p).wait()
        rows = piece_of(early, 0, p)
        wide = rows[...].astype(jnp.float32)
        inverse = lax.rsqrt(jnp.sum(wide * wide, axis=1, keepdims=True) + EPS)
        rows[...] = (wide * inverse).astype(jnp.bfloat16)

    best[...] = jnp.full(best.shape, FILL, jnp.float32)
    normalize(0)
    pl.semaphore_wait(barrier, 3 + 3 * hub_f)

    x_from = 1 - hub_f
    def send_own(p):
        piece = piece_of(early, 0, p)

        @pl.when(hub)
        def _():
            for q in range(PER):
                chunk = p * PER + q
                remote(chunk_of(early, 0, chunk), chunk_of(early, 2, chunk), own_send.at[2], e2_recv.at[chunk], up).start()
            remote(piece, piece_of(early, 3, p), own_send.at[3], one_recv.at[0], down).start()

            @pl.when(is_a)
            def _():
                remote(piece, piece_of(early, 4, p), own_send.at[4], one_recv.at[1], beside).start()

        @pl.when(hub_f == 0)
        def _():
            remote(piece, piece_of(early, 1, p), own_send.at[2], e1_recv.at[p], beside).start()

        for h in range(2):
            src = half_of(early, 0, p, h)
            remote(src, half_of(late_a, x_from, p, h), own_send.at[0], late_recv.at[x_from, p, h], x_up).start()
            remote(src, half_of(late_b, x_from, p, h), own_send.at[1], late_recv.at[2 + x_from, p, h], x_down).start()

        @pl.when(hub)
        def _():
            remote(piece, piece_of(early, 1, p), own_send.at[5], one_recv.at[2], mate).start()

    def across_early(chunk):
        src = chunk_of(early, 2, chunk)
        arrived(src, e2_recv.at[chunk])

        @pl.when(is_b)
        def _():
            remote(src, chunk_of(early, 4, chunk), own_send.at[4], one_recv.at[1], beside).start()

    meta_copy(meta_e.at[0], meta_l.at[x_from], LATE + x_from, 0, x_up).start()
    meta_copy(meta_e.at[0], meta_l.at[2 + x_from], LATE + 2 + x_from, 1, x_down).start()

    @pl.when(hub)
    def _():
        meta_copy(meta_e.at[0], meta_e.at[2], 2, 2, up).start()
        meta_copy(meta_e.at[0], meta_e.at[3], 3, 3, down).start()
        meta_copy(meta_e.at[0], meta_e.at[1], 1, 4, mate).start()

        @pl.when(is_a)
        def _():
            meta_copy(meta_e.at[0], meta_e.at[4], 4, 5, beside).start()

    @pl.when(hub_f == 0)
    def _():
        meta_copy(meta_e.at[0], meta_e.at[1], 1, 2, beside).start()

    send_own(0)

    def rest(p, carry):
        normalize(p)
        send_own(p)

        @pl.when(hub & (p >= PIECES - PER))
        def _():
            across_early(p - (PIECES - PER))
        return carry

    lax.fori_loop(1, PIECES, rest, 0)

    copies = [pltpu.make_async_copy(meta_e.at[item, BLOCKS], tabs.at[item], tab_sem.at[item]) for item in range(5)]
    copies += [pltpu.make_async_copy(meta_l.at[item, BLOCKS], tabs.at[LATE + item], tab_sem.at[LATE + item])
               for item in range(4)]

    @pl.when(hub)
    def _():
        arrived(meta_e.at[1], meta_recv.at[1])
        meta_copy(meta_e.at[1], meta_l.at[0], LATE, 6, up).start()
        meta_copy(meta_e.at[1], meta_l.at[1], LATE + 1, 7, down).start()

        @pl.when(is_a)
        def _():
            meta_copy(meta_e.at[1], meta_l.at[2], LATE + 2, 8, beside).start()

        arrived(meta_e.at[2], meta_recv.at[2])

        @pl.when(is_b)
        def _():
            meta_copy(meta_e.at[2], meta_e.at[4], 4, 5, beside).start()

        def take(p, carry):
            @pl.when(p < PIECES - 1)
            def _():
                for q in range(PER):
                    across_early((p + 1) * PER + q)

            piece = piece_of(early, 1, p)
            arrived(piece, e1_recv.at[p])
            for q in range(PER):
                chunk = p * PER + q
                remote(chunk_of(early, 1, chunk), chunk_of(late_a, 0, chunk), fwd_send.at[0], l0_recv.at[chunk], up).start()
            for h in range(2):
                src = half_of(early, 1, p, h)
                remote(src, half_of(late_a, 1, p, h), fwd_send.at[1], late_recv.at[1, p, h], down).start()

            @pl.when(is_a)
            def _():
                for h in range(2):
                    src = half_of(early, 1, p, h)
                    remote(src, half_of(late_b, 0, p, h), fwd_send.at[2], late_recv.at[2, p, h], beside).start()
            return carry

        lax.fori_loop(0, PIECES, take, 0)
        arrived(meta_l.at[0], meta_recv.at[LATE])

        @pl.when(is_b)
        def _():
            meta_copy(meta_l.at[0], meta_l.at[2], LATE + 2, 8, beside).start()

    @pl.when(hub_f == 0)
    def _():
        arrived(early.at[1], one_recv.at[2])
        arrived(meta_e.at[1], meta_recv.at[1])
        for item in range(4):
            arrived(meta_l.at[item], meta_recv.at[LATE + item])
        for copy in copies:
            copy.start()
        for copy in copies:
            copy.wait()

    def by_role(for_hub, for_clus):
        return for_clus + (for_hub - for_clus) * hub_f

    def lists(for_hub, for_clus):
        fields = []
        for f in range(2):
            ours, theirs = packed([e[f] for e in for_hub], 3), packed([e[f] for e in for_clus], 3)
            fields.append([by_role(ours[w], theirs[w]) for w in range(2)])
        return fields + [by_role(flags([e[2] == 1 for e in for_hub]), flags([e[2] == 1 for e in for_clus]))]

    todo = (lists(EE_HUB, EE_CLUS), lists(EL_HUB, EL_CLUS), lists(LL_HUB, LL_CLUS))
    offsets = []
    for f in range(2):
        a, b, c_ = (packed([p[f] for p in place], 2)[0] for place in (PLACE_A, PLACE_B, PLACE_C))
        offsets.append(by_role(a + (b - a) * (yy % 2), c_))

    line = lax.broadcasted_iota(jnp.int32, (16, 128), 0)
    block_at = line // 4

    def look_up(kind, at):
        second_word = at // WORD
        shift = 3 * (at - WORD * second_word)
        row, col = (((words[0] + (words[1] - words[0]) * second_word) >> shift) & 7 for words in todo[kind][:2])
        asks = (todo[kind][2] >> at) & 1
        row_item = row + (LATE if kind == 2 else 0)
        col_item = col + (LATE if kind > 0 else 0)
        asker = row_item + (col_item - row_item) * asks
        other = row_item + col_item - asker
        first, second = ((offset >> (2 * other)) & 3 for offset in offsets)
        place_c = ((x + first) % 4) * 2 + (k + second) % 2
        place_g = 8 + ((z + first) % 4) * 4 + (y + second) % 4
        in_grp = hub_f
        if kind == 0:
            own_pair = 1 - jnp.minimum(at // 2, 1)
            in_grp = own_pair * at + (1 - own_pair) * hub_f
        place = in_grp * place_g + (1 - in_grp) * place_c
        return row, col, row_item, col_item, tabs[asker, asks, place], tabs[asker, 1 - asks, place], tabs[asker, 2, place]

    def labels_down(meta, item, block):
        labs = [meta[item, block, i:i + 1, :].astype(jnp.float32) for i in range(4)]
        return [jnp.transpose(jnp.broadcast_to(lab, (128, 128))) for lab in labs]

    def raise_best(item, values, where):
        best[item] = jnp.maximum(best[item], jnp.where(where, values, FILL))

    def full(scalar):
        return jnp.full((16, 128), scalar, jnp.int32)

    def product(rows, cols):
        return lax.dot_general(rows, cols, (((1,), (1,)), ((), ())), preferred_element_type=jnp.float32)

    def score(cosine, row_labs, col_labs, off, row_best, col_best):
        for j, col_lab in enumerate(col_labs):
            line_best = None
            for i in range(4):
                tile = cosine[i * 128:(i + 1) * 128, j * 128:(j + 1) * 128]
                keep = row_labs[i] == col_lab
                if off is not None and i == len(col_best):
                    keep = keep & off
                tile = jnp.where(keep, tile, FILL)
                row_best[i] = tile if row_best[i] is None else jnp.maximum(row_best[i], tile)
                folded = jnp.max(tile.reshape(16, 8, 128), axis=0)
                line_best = folded if line_best is None else jnp.maximum(line_best, folded)
            col_best.append(jnp.max(line_best, axis=0, keepdims=True))

    def down_rows(row_best):
        return jnp.concatenate([jnp.max(jnp.transpose(t), axis=0, keepdims=True) for t in row_best] * 4, axis=0)

    def pair(kind, at):
        row, col, row_item, col_item, row_block, col_block, alive = look_up(kind, at)
        row_ref, row_meta = (late_a, meta_l) if kind == 2 else (early, meta_e)
        col_ref, col_meta = (late_a if at == 0 else late_b, meta_l) if kind == 2 else (early, meta_e)
        col_at = col - 2 if kind == 2 and at > 0 else col
        rows = row_ref[row, row_block]
        row_labs = labels_down(row_meta, row, row_block)
        col_labs = [col_meta[col, col_block, i:i + 1, :].astype(jnp.float32) for i in range(4)]
        off = None
        if kind == 0:
            apart = jnp.where((row == col) & (row_block == col_block), 0, 1)
            off = (lax.broadcasted_iota(jnp.int32, (128, 128), 0) != lax.broadcasted_iota(jnp.int32, (128, 128), 1))
            off = off | (jnp.full((128, 128), apart, jnp.int32) > 0)
        row_best, col_best = [None] * 4, []
        for n in range(2):
            cols = col_ref[col_at, col_block, n * PIECE:(n + 1) * PIECE, :]
            score(product(rows, cols), row_labs, col_labs[2 * n:2 * n + 2], off, row_best, col_best)
        raise_best(row_item, down_rows(row_best), (block_at == row_block) & (full(alive) > 0))
        raise_best(col_item, jnp.concatenate(col_best * 4, axis=0), (block_at == col_block) & (full(alive) > 0))

    def first_half(at, p):
        row, col, _, _, row_block, _, _ = look_up(1, at)
        cols = half_of(late_a, col, p, 0) if at < EL_A else half_of(late_b, col - 2, p, 0)
        part[at] = product(early[row, row_block, :, :HALF], cols[...])

    def late_pair(at, p, halved=False):
        row, col, row_item, col_item, row_block, col_block, alive = look_up(1, at)
        block, half = p // 2, p % 2
        row_labs = labels_down(meta_e, row, row_block)
        col_labs = [meta_l[col, block, pl.ds(half * 2 + j, 1), :].astype(jnp.float32) for j in range(2)]
        row_best, col_best = [None] * 4, []
        late, late_at = (late_a, col) if at < EL_A else (late_b, col - 2)
        if halved:
            cosine = part[at] + product(early[row, row_block, :, HALF:], half_of(late, late_at, p, 1)[...])
        else:
            cosine = product(early[row, row_block], piece_of(late, late_at, p)[...])
        score(cosine, row_labs, col_labs, None, row_best, col_best)
        asked = full(jnp.where(col_block == block, alive, 0)) > 0
        raise_best(row_item, down_rows(row_best), (block_at == row_block) & asked)
        at_line = block * 4 + half * 2
        both = jnp.where(line == at_line, col_best[0], col_best[1])
        raise_best(col_item, both, asked & ((line == at_line) | (line == at_line + 1)))

    in_b = yy % 2
    aside = 3 - 2 * in_b
    hub_owners = [(0, dev(0, k, 0, aside)), (0, dev(0, k, 3, 0)), (1, dev(0, k, 1, 0)),
                  (2, dev(0, k, 3 - 3 * in_b, 1 + 2 * in_b)), (1, dev(0, k, 3, aside)), (2, dev(0, k, 1, aside)),
                  (3, dev(0, k, 3 - 3 * in_b, 2))]

    def pass_on(p, q):
        chunk = p * PER + q

        @pl.when(hub)
        def _():
            src = chunk_of(late_a, 0, chunk)
            arrived(src, l0_recv.at[chunk])

            @pl.when(is_b)
            def _():
                remote(src, chunk_of(late_b, 0, chunk), fwd_send.at[2], late_recv.at[2, p, q // 2], beside).start()

    early_pairs = len(EE_CLUS) + (len(EE_HUB) - 4 - len(EE_CLUS)) * hub_f

    def late_a_landed(p, h):
        arrived(half_of(late_a, 1, p, h), late_recv.at[1, p, h])

        @pl.when(hub_f == 0)
        def _():
            arrived(half_of(late_a, 0, p, h), late_recv.at[0, p, h])

    def late_b_landed(p, h):
        arrived(half_of(late_b, 0, p, h), late_recv.at[2, p, h])

        @pl.when(hub_f == 0)
        def _():
            arrived(half_of(late_b, 1, p, h), late_recv.at[3, p, h])

    def late_a_pairs(p):
        for h in range(2):
            late_a_landed(p, h)
        for at in range(EL_A):
            late_pair(at, p)

    def late_b_pairs(p):
        for h in range(2):
            late_b_landed(p, h)
        for at in range(EL_A, len(EL_HUB)):
            late_pair(at, p)

    def step(p, carry):
        pass_on(p, 0)

        @pl.when(hub & (p == 0))
        def _():
            arrived(early.at[3], one_recv.at[0])
            arrived(early.at[4], one_recv.at[1])
            for item in (3, 4):
                arrived(meta_e.at[item], meta_recv.at[item])
            for item in (1, 2):
                arrived(meta_l.at[item], meta_recv.at[LATE + item])
            for copy in copies:
                copy.start()
            for copy in copies:
                copy.wait()

        @pl.when(2 * p < early_pairs)
        def _():
            pair(0, 2 * p)
            pair(0, 2 * p + 1)

        pass_on(p, 1)

        @pl.when(p > 0)
        def _():
            late_a_pairs(p - 1)

        @pl.when(hub & (p == 0))
        def _():
            pair(0, 16)
            pair(0, 17)

        pass_on(p, 2)

        @pl.when(p > 0)
        def _():
            late_b_pairs(p - 1)

        @pl.when(hub & (p == 0))
        def _():
            pair(0, 14)
            pair(0, 15)

        pass_on(p, 3)
        return carry

    lax.fori_loop(0, PIECES - 1, step, 0)
    last = PIECES - 1
    pass_on(last, 0)
    late_a_pairs(last - 1)
    pass_on(last, 1)
    late_b_pairs(last - 1)
    pass_on(last, 2)
    late_a_landed(last, 0)
    for at in range(EL_A):
        first_half(at, last)
    pass_on(last, 3)
    late_b_landed(last, 0)
    for at in range(EL_A, len(EL_HUB)):
        first_half(at, last)
    late_a_landed(last, 1)
    for at in range(EL_A):
        late_pair(at, last, True)
    late_b_landed(last, 1)
    for at in range(EL_A, len(EL_HUB)):
        late_pair(at, last, True)
    for at in range(3):
        pair(2, at)

    @pl.when(hub_f == 0)
    def _():
        pair(2, 3)
        pair(2, 4)

    def give(item, to, send, device):
        return remote(best.at[item], ret.at[to], ret_send.at[send], ret_recv.at[to], device)

    def hub_gives():
        return [give(item, to, item - 1, device) for item, (to, device) in enumerate(hub_owners, 1)]

    def clus_gives():
        return [give(1, 3, 0, mate), give(5, 4, 1, dev(3, 1 - k, 0, 0)), give(6, 4, 2, dev(3, k, 0, 0)),
                give(7, 5, 3, dev(1, 1 - k, 0, 0)), give(8, 5, 4, dev(1, k, 0, 0))]

    for which, gives in ((hub, hub_gives), (hub_f == 0, clus_gives)):
        @pl.when(which)
        def _(gives=gives):
            for copy in reversed(gives()):
                copy.start()

    for s in range(2):
        arrived(early.at[0], own_send.at[s])
        arrived(meta_e.at[0], meta_send.at[s])

    @pl.when(hub)
    def _():
        for s in range(2, 6):
            arrived(early.at[0], own_send.at[s])
        for s in range(3):
            arrived(early.at[0], fwd_send.at[s])
        for s in range(2, 9):
            arrived(meta_e.at[0], meta_send.at[s])
        for s in range(7):
            arrived(best.at[0], ret_send.at[s])

    @pl.when(hub_f == 0)
    def _():
        arrived(early.at[0], own_send.at[2])
        arrived(meta_e.at[0], meta_send.at[2])
        for s in range(5):
            arrived(best.at[0], ret_send.at[s])

    result = best[0]
    for j in range(6):
        arrived(ret.at[j], ret_recv.at[j])
        result = jnp.maximum(result, ret[j])
    out[...] = result


def on_device(embeddings, labels, partner_block, own_block, live):
    dma = pltpu.SemaphoreType.DMA
    vmem = pl.BlockSpec(memory_space=pltpu.VMEM)
    best = pl.pallas_call(
        kernel,
        out_shape=jax.ShapeDtypeStruct((16, 128), jnp.float32),
        in_specs=[pl.BlockSpec(memory_space=pl.ANY)] * 5,
        out_specs=vmem,
        scratch_shapes=[
            pltpu.VMEM((5, BLOCKS, BLOCK, D), jnp.bfloat16),
            pltpu.VMEM((2, BLOCKS, BLOCK, D), jnp.bfloat16),
            pltpu.VMEM((2, BLOCKS, BLOCK, D), jnp.bfloat16),
            pltpu.VMEM((16, 128), jnp.int32),
            pltpu.VMEM((3, 1, 24), jnp.int32),
            pltpu.VMEM((5, BLOCKS + 1, 8, 128), jnp.int32),
            pltpu.VMEM((4, BLOCKS + 1, 8, 128), jnp.int32),
            pltpu.SMEM((9, 8, 128), jnp.int32),
            pltpu.VMEM((9, 16, 128), jnp.float32),
            pltpu.VMEM((len(EL_HUB), BLOCK, PIECE), jnp.float32),
            pltpu.VMEM((6, 16, 128), jnp.float32),
            dma((PIECES + 4,)), dma((9,)), dma((6,)), dma((3,)), dma((9,)), dma((7,)),
            dma((PIECES,)), dma((CHUNKS,)), dma((CHUNKS,)), dma((4, PIECES, 2)), dma((3,)), dma((9,)), dma((6,)),
        ],
        compiler_params=pltpu.CompilerParams(collective_id=0, has_side_effects=True, vmem_limit_bytes=56 << 20),
        cost_estimate=pl.CostEstimate(flops=24 * 2 * 512 * 512 * 1024, bytes_accessed=4 << 20, transcendentals=2048),
    )(embeddings, labels.reshape(16, 128), own_block, partner_block, live)
    return best.reshape(2048)


def solution(mesh):
    placed = (
        P(("clus", "grp"), None),
        P(("clus", "grp")),
        P(("clus", "grp"), None),
        P(("clus", "grp"), None),
        P(("clus", "grp"), None),
    )
    return jax.shard_map(
        on_device, mesh=mesh, in_specs=placed, out_specs=P(("clus", "grp")), check_vma=False
    )
```

```python
import jax
import jax.numpy as jnp
from jax import lax
from jax.experimental import pallas as pl
from jax.experimental.pallas import tpu as pltpu
from jax.sharding import PartitionSpec as P

MESH = pl.DeviceIdType.MESH
ROWS = 2048
D = 1024
BLOCK = 512
BLOCKS = ROWS // BLOCK
EPS = 1e-06
FILL = -1.0

PIECE = 256
PIECES = ROWS // PIECE
PER = 4
CHUNKS = PIECES * PER
WIDTH = D // PER
HALF = D // 2

EE_HUB = [(0, 0, 0), (0, 0, 0), (0, 1, 0), (0, 1, 1), (0, 2, 0), (0, 3, 0), (2, 3, 0), (1, 2, 0), (1, 2, 1),
          (1, 3, 0), (1, 3, 1), (0, 4, 0), (0, 4, 1), (1, 4, 0), (1, 4, 1), (3, 4, 0), (3, 4, 1), (3, 4, 1)]
EL_HUB = [(1, 0, 0), (1, 1, 0), (2, 1, 0), (2, 1, 1), (4, 1, 0), (4, 1, 1), (3, 2, 0), (3, 2, 1),
          (0, 2, 0), (0, 2, 1), (1, 2, 0), (1, 2, 1)]
LL_HUB = [(0, 1, 0), (1, 2, 0), (1, 2, 1), (1, 2, 1), (1, 2, 1)]
EE_CLUS = [(0, 0, 0), (0, 0, 0), (0, 1, 0), (0, 1, 1)]
EL_CLUS = [(0, 1, 0), (0, 1, 1), (1, 0, 0), (1, 0, 1), (0, 1, 0), (0, 1, 1),
           (0, 2, 0), (0, 2, 1), (1, 3, 0), (1, 3, 1), (0, 2, 0), (0, 2, 1)]
LL_CLUS = [(0, 1, 0), (0, 2, 0), (0, 3, 0), (1, 2, 0), (1, 3, 0)]
EL_A = 6
PLACE_A = [(0, 0), (0, 3), (3, 0), (1, 0), (3, 1), (3, 3), (1, 3), (3, 2), (0, 0)]
PLACE_B = [(0, 0), (0, 1), (3, 0), (1, 0), (0, 3), (3, 1), (1, 1), (0, 2), (0, 0)]
PLACE_C = [(0, 0), (0, 1), (0, 0), (0, 0), (0, 0), (3, 1), (3, 0), (1, 1), (1, 0)]
LATE = 5
WORD = 9


def packed(values, bits):
    words = [0, 0]
    for at, value in enumerate(values):
        words[at // WORD] |= value << bits * (at % WORD)
    return words


def flags(values):
    return sum(int(value) << at for at, value in enumerate(values))


def kernel(emb, labs_in, own_in, part_in, live_in, out, early, late_a, late_b, labs, small, meta_e, meta_l, tabs, best, part, ret,
           in_sem, tab_sem, own_send, fwd_send, meta_send, ret_send,
           e1_recv, e2_recv, l0_recv, late_recv, one_recv, meta_recv, ret_recv):
    c = lax.axis_index("clus")
    g = lax.axis_index("grp")
    x, k = c // 2, c % 2
    z, y = g // 4, g % 4
    yy = (y + 2 * k) % 4
    hub = yy < 2
    hub_f = 1 - yy // 2
    is_a, is_b = yy == 0, yy == 1
    kc = 1 - y // 2

    def dev(dx, core, dz, dy):
        return (((x + dx) % 4) * 2 + core, ((z + dz) % 4) * 4 + (y + dy) % 4)

    up, down = dev(0, k, 1, 0), dev(0, k, 3, 0)
    mate = dev(0, 1 - k, 0, 0)
    x_up, x_down = dev(1, kc, 0, 0), dev(3, kc, 0, 0)
    beside = dev(0, k, 0, 1 + 2 * ((yy + 1) // 2 % 2))

    barrier = pltpu.get_barrier_semaphore()

    def greet(*devices):
        for device in devices:
            pl.semaphore_signal(barrier, inc=1, device_id=device, device_id_type=MESH)

    @pl.when(hub)
    def _():
        greet(up, down, beside, dev(0, k, 0, 3 - 2 * (yy % 2)))

    @pl.when(hub_f == 0)
    def _():
        greet(mate, x_up, x_down, dev(1, 1 - k, 0, 0), dev(3, 1 - k, 0, 0))

    def part_of(ref, item, at, size):
        per = BLOCK // size
        return ref.at[item, at // per, pl.ds(pl.multiple_of(at % per * size, size), size)]

    def piece_of(ref, item, p):
        return part_of(ref, item, p, PIECE)

    def slab_of(ref, item, p, first, width):
        rows = pl.ds(pl.multiple_of(p % 2 * PIECE, PIECE), PIECE)
        return ref.at[item, p // 2, rows, pl.ds(pl.multiple_of(first, width), width)]

    def chunk_of(ref, item, chunk):
        return slab_of(ref, item, chunk // PER, chunk % PER * WIDTH, WIDTH)

    def half_of(ref, item, p, h):
        return slab_of(ref, item, p, h * HALF, HALF)

    def piece_in(p):
        return pltpu.make_async_copy(emb.at[pl.ds(p * PIECE, PIECE)], piece_of(early, 0, p), in_sem.at[p])

    into = [pltpu.make_async_copy(labs_in, labs, in_sem.at[PIECES])]
    into += [pltpu.make_async_copy(tab, small.at[at], in_sem.at[PIECES + 1 + at])
             for at, tab in enumerate((own_in, part_in, live_in))]
    piece_in(0).start()
    for copy in into:
        copy.start()
    for p in range(1, PIECES):
        piece_in(p).start()
    for copy in into:
        copy.wait()
    for b in range(BLOCKS):
        meta_e[0, b, 0:4, :] = labs[4 * b:4 * b + 4, :]
    for at in range(3):
        meta_e[0, BLOCKS, at:at + 1, 0:24] = small[at]

    def remote(src, dst, send, recv, device):
        return pltpu.make_async_remote_copy(src_ref=src, dst_ref=dst, send_sem=send, recv_sem=recv,
                                            device_id=device, device_id_type=MESH)

    def arrived(ref, sem):
        pltpu.make_async_copy(ref, ref, sem).wait()

    def meta_copy(src, dst, item, send, device):
        return remote(src, dst, meta_send.at[send], meta_recv.at[item], device)

    def normalize(p):
        piece_in(p).wait()
        rows = piece_of(early, 0, p)
        wide = rows[...].astype(jnp.float32)
        inverse = lax.rsqrt(jnp.sum(wide * wide, axis=1, keepdims=True) + EPS)
        rows[...] = (wide * inverse).astype(jnp.bfloat16)

    best[...] = jnp.full(best.shape, FILL, jnp.float32)
    normalize(0)
    pl.semaphore_wait(barrier, 3 + 3 * hub_f)

    x_from = 1 - hub_f
    def send_own(p):
        piece = piece_of(early, 0, p)

        @pl.when(hub)
        def _():
            for q in range(PER):
                chunk = p * PER + q
                remote(chunk_of(early, 0, chunk), chunk_of(early, 2, chunk), own_send.at[2], e2_recv.at[chunk], up).start()
            remote(piece, piece_of(early, 3, p), own_send.at[3], one_recv.at[0], down).start()

            @pl.when(is_a)
            def _():
                remote(piece, piece_of(early, 4, p), own_send.at[4], one_recv.at[1], beside).start()

        @pl.when(hub_f == 0)
        def _():
            remote(piece, piece_of(early, 1, p), own_send.at[2], e1_recv.at[p], beside).start()

        for h in range(2):
            src = half_of(early, 0, p, h)
            remote(src, half_of(late_a, x_from, p, h), own_send.at[0], late_recv.at[x_from, p, h], x_up).start()
            remote(src, half_of(late_b, x_from, p, h), own_send.at[1], late_recv.at[2 + x_from, p, h], x_down).start()

        @pl.when(hub)
        def _():
            remote(piece, piece_of(early, 1, p), own_send.at[5], one_recv.at[2], mate).start()

    def across_early(chunk):
        src = chunk_of(early, 2, chunk)
        arrived(src, e2_recv.at[chunk])

        @pl.when(is_b)
        def _():
            remote(src, chunk_of(early, 4, chunk), own_send.at[4], one_recv.at[1], beside).start()

    meta_copy(meta_e.at[0], meta_l.at[x_from], LATE + x_from, 0, x_up).start()
    meta_copy(meta_e.at[0], meta_l.at[2 + x_from], LATE + 2 + x_from, 1, x_down).start()

    @pl.when(hub)
    def _():
        meta_copy(meta_e.at[0], meta_e.at[2], 2, 2, up).start()
        meta_copy(meta_e.at[0], meta_e.at[3], 3, 3, down).start()
        meta_copy(meta_e.at[0], meta_e.at[1], 1, 4, mate).start()

        @pl.when(is_a)
        def _():
            meta_copy(meta_e.at[0], meta_e.at[4], 4, 5, beside).start()

    @pl.when(hub_f == 0)
    def _():
        meta_copy(meta_e.at[0], meta_e.at[1], 1, 2, beside).start()

    send_own(0)

    def rest(p, carry):
        normalize(p)
        send_own(p)

        @pl.when(hub & (p >= PIECES - PER))
        def _():
            across_early(p - (PIECES - PER))
        return carry

    lax.fori_loop(1, PIECES, rest, 0)

    copies = [pltpu.make_async_copy(meta_e.at[item, BLOCKS], tabs.at[item], tab_sem.at[item]) for item in range(5)]
    copies += [pltpu.make_async_copy(meta_l.at[item, BLOCKS], tabs.at[LATE + item], tab_sem.at[LATE + item])
               for item in range(4)]

    @pl.when(hub)
    def _():
        arrived(meta_e.at[1], meta_recv.at[1])
        meta_copy(meta_e.at[1], meta_l.at[0], LATE, 6, up).start()
        meta_copy(meta_e.at[1], meta_l.at[1], LATE + 1, 7, down).start()

        @pl.when(is_a)
        def _():
            meta_copy(meta_e.at[1], meta_l.at[2], LATE + 2, 8, beside).start()

        arrived(meta_e.at[2], meta_recv.at[2])

        @pl.when(is_b)
        def _():
            meta_copy(meta_e.at[2], meta_e.at[4], 4, 5, beside).start()

        def take(p, carry):
            @pl.when(p < PIECES - 1)
            def _():
                for q in range(PER):
                    across_early((p + 1) * PER + q)

            piece = piece_of(early, 1, p)
            arrived(piece, e1_recv.at[p])
            for q in range(PER):
                chunk = p * PER + q
                remote(chunk_of(early, 1, chunk), chunk_of(late_a, 0, chunk), fwd_send.at[0], l0_recv.at[chunk], up).start()
            for h in range(2):
                src = half_of(early, 1, p, h)
                remote(src, half_of(late_a, 1, p, h), fwd_send.at[1], late_recv.at[1, p, h], down).start()

            @pl.when(is_a)
            def _():
                for h in range(2):
                    src = half_of(early, 1, p, h)
                    remote(src, half_of(late_b, 0, p, h), fwd_send.at[2], late_recv.at[2, p, h], beside).start()
            return carry

        lax.fori_loop(0, PIECES, take, 0)
        arrived(meta_l.at[0], meta_recv.at[LATE])

        @pl.when(is_b)
        def _():
            meta_copy(meta_l.at[0], meta_l.at[2], LATE + 2, 8, beside).start()

    @pl.when(hub_f == 0)
    def _():
        arrived(early.at[1], one_recv.at[2])
        arrived(meta_e.at[1], meta_recv.at[1])
        for item in range(4):
            arrived(meta_l.at[item], meta_recv.at[LATE + item])
        for copy in copies:
            copy.start()
        for copy in copies:
            copy.wait()

    def by_role(for_hub, for_clus):
        return for_clus + (for_hub - for_clus) * hub_f

    def lists(for_hub, for_clus):
        fields = []
        for f in range(2):
            ours, theirs = packed([e[f] for e in for_hub], 3), packed([e[f] for e in for_clus], 3)
            fields.append([by_role(ours[w], theirs[w]) for w in range(2)])
        return fields + [by_role(flags([e[2] == 1 for e in for_hub]), flags([e[2] == 1 for e in for_clus]))]

    todo = (lists(EE_HUB, EE_CLUS), lists(EL_HUB, EL_CLUS), lists(LL_HUB, LL_CLUS))
    offsets = []
    for f in range(2):
        a, b, c_ = (packed([p[f] for p in place], 2)[0] for place in (PLACE_A, PLACE_B, PLACE_C))
        offsets.append(by_role(a + (b - a) * (yy % 2), c_))

    line = lax.broadcasted_iota(jnp.int32, (16, 128), 0)
    block_at = line // 4

    def look_up(kind, at):
        second_word = at // WORD
        shift = 3 * (at - WORD * second_word)
        row, col = (((words[0] + (words[1] - words[0]) * second_word) >> shift) & 7 for words in todo[kind][:2])
        asks = (todo[kind][2] >> at) & 1
        row_item = row + (LATE if kind == 2 else 0)
        col_item = col + (LATE if kind > 0 else 0)
        asker = row_item + (col_item - row_item) * asks
        other = row_item + col_item - asker
        first, second = ((offset >> (2 * other)) & 3 for offset in offsets)
        place_c = ((x + first) % 4) * 2 + (k + second) % 2
        place_g = 8 + ((z + first) % 4) * 4 + (y + second) % 4
        in_grp = hub_f
        if kind == 0:
            own_pair = 1 - jnp.minimum(at // 2, 1)
            in_grp = own_pair * at + (1 - own_pair) * hub_f
        place = in_grp * place_g + (1 - in_grp) * place_c
        return row, col, row_item, col_item, tabs[asker, asks, place], tabs[asker, 1 - asks, place], tabs[asker, 2, place]

    def labels_down(meta, item, block):
        labs = [meta[item, block, i:i + 1, :].astype(jnp.float32) for i in range(4)]
        return [jnp.transpose(jnp.broadcast_to(lab, (128, 128))) for lab in labs]

    def raise_best(item, values, where):
        best[item] = jnp.maximum(best[item], jnp.where(where, values, FILL))

    def full(scalar):
        return jnp.full((16, 128), scalar, jnp.int32)

    def product(rows, cols):
        return lax.dot_general(rows, cols, (((1,), (1,)), ((), ())), preferred_element_type=jnp.float32)

    def score(cosine, row_labs, col_labs, off, row_best, col_best):
        for j, col_lab in enumerate(col_labs):
            line_best = None
            for i in range(4):
                tile = cosine[i * 128:(i + 1) * 128, j * 128:(j + 1) * 128]
                keep = row_labs[i] == col_lab
                if off is not None and i == len(col_best):
                    keep = keep & off
                tile = jnp.where(keep, tile, FILL)
                row_best[i] = tile if row_best[i] is None else jnp.maximum(row_best[i], tile)
                folded = jnp.max(tile.reshape(16, 8, 128), axis=0)
                line_best = folded if line_best is None else jnp.maximum(line_best, folded)
            col_best.append(jnp.max(line_best, axis=0, keepdims=True))

    def down_rows(row_best):
        return jnp.concatenate([jnp.max(jnp.transpose(t), axis=0, keepdims=True) for t in row_best] * 4, axis=0)

    def pair(kind, at):
        row, col, row_item, col_item, row_block, col_block, alive = look_up(kind, at)
        row_ref, row_meta = (late_a, meta_l) if kind == 2 else (early, meta_e)
        col_ref, col_meta = (late_a if at == 0 else late_b, meta_l) if kind == 2 else (early, meta_e)
        col_at = col - 2 if kind == 2 and at > 0 else col
        rows = row_ref[row, row_block]
        row_labs = labels_down(row_meta, row, row_block)
        col_labs = [col_meta[col, col_block, i:i + 1, :].astype(jnp.float32) for i in range(4)]
        off = None
        if kind == 0:
            apart = jnp.where((row == col) & (row_block == col_block), 0, 1)
            off = (lax.broadcasted_iota(jnp.int32, (128, 128), 0) != lax.broadcasted_iota(jnp.int32, (128, 128), 1))
            off = off | (jnp.full((128, 128), apart, jnp.int32) > 0)
        row_best, col_best = [None] * 4, []
        for n in range(2):
            cols = col_ref[col_at, col_block, n * PIECE:(n + 1) * PIECE, :]
            score(product(rows, cols), row_labs, col_labs[2 * n:2 * n + 2], off, row_best, col_best)
        raise_best(row_item, down_rows(row_best), (block_at == row_block) & (full(alive) > 0))
        raise_best(col_item, jnp.concatenate(col_best * 4, axis=0), (block_at == col_block) & (full(alive) > 0))

    def first_half(at, p):
        row, col, _, _, row_block, _, _ = look_up(1, at)
        cols = half_of(late_a, col, p, 0) if at < EL_A else half_of(late_b, col - 2, p, 0)
        part[at] = product(early[row, row_block, :, :HALF], cols[...])

    def late_pair(at, p, halved=False):
        row, col, row_item, col_item, row_block, col_block, alive = look_up(1, at)
        block, half = p // 2, p % 2
        row_labs = labels_down(meta_e, row, row_block)
        col_labs = [meta_l[col, block, pl.ds(half * 2 + j, 1), :].astype(jnp.float32) for j in range(2)]
        row_best, col_best = [None] * 4, []
        late, late_at = (late_a, col) if at < EL_A else (late_b, col - 2)
        if halved:
            cosine = part[at] + product(early[row, row_block, :, HALF:], half_of(late, late_at, p, 1)[...])
        else:
            cosine = product(early[row, row_block], piece_of(late, late_at, p)[...])
        score(cosine, row_labs, col_labs, None, row_best, col_best)
        asked = full(jnp.where(col_block == block, alive, 0)) > 0
        raise_best(row_item, down_rows(row_best), (block_at == row_block) & asked)
        at_line = block * 4 + half * 2
        both = jnp.where(line == at_line, col_best[0], col_best[1])
        raise_best(col_item, both, asked & ((line == at_line) | (line == at_line + 1)))

    in_b = yy % 2
    aside = 3 - 2 * in_b
    hub_owners = [(0, dev(0, k, 0, aside)), (0, dev(0, k, 3, 0)), (1, dev(0, k, 1, 0)),
                  (2, dev(0, k, 3 - 3 * in_b, 1 + 2 * in_b)), (1, dev(0, k, 3, aside)), (2, dev(0, k, 1, aside)),
                  (3, dev(0, k, 3 - 3 * in_b, 2))]

    def pass_on(p, q):
        chunk = p * PER + q

        @pl.when(hub)
        def _():
            src = chunk_of(late_a, 0, chunk)
            arrived(src, l0_recv.at[chunk])

            @pl.when(is_b)
            def _():
                remote(src, chunk_of(late_b, 0, chunk), fwd_send.at[2], late_recv.at[2, p, q // 2], beside).start()

    early_pairs = len(EE_CLUS) + (len(EE_HUB) - 4 - len(EE_CLUS)) * hub_f

    def late_a_landed(p, h):
        arrived(half_of(late_a, 1, p, h), late_recv.at[1, p, h])

        @pl.when(hub_f == 0)
        def _():
            arrived(half_of(late_a, 0, p, h), late_recv.at[0, p, h])

    def late_b_landed(p, h):
        arrived(half_of(late_b, 0, p, h), late_recv.at[2, p, h])

        @pl.when(hub_f == 0)
        def _():
            arrived(half_of(late_b, 1, p, h), late_recv.at[3, p, h])

    def late_a_pairs(p):
        for h in range(2):
            late_a_landed(p, h)
        for at in range(EL_A):
            late_pair(at, p)

    def late_b_pairs(p):
        for h in range(2):
            late_b_landed(p, h)
        for at in range(EL_A, len(EL_HUB)):
            late_pair(at, p)

    def step(p, carry):
        pass_on(p, 0)

        @pl.when(hub & (p == 0))
        def _():
            arrived(early.at[3], one_recv.at[0])
            arrived(early.at[4], one_recv.at[1])
            for item in (3, 4):
                arrived(meta_e.at[item], meta_recv.at[item])
            for item in (1, 2):
                arrived(meta_l.at[item], meta_recv.at[LATE + item])
            for copy in copies:
                copy.start()
            for copy in copies:
                copy.wait()

        @pl.when(2 * p < early_pairs)
        def _():
            pair(0, 2 * p)
            pair(0, 2 * p + 1)

        pass_on(p, 1)

        @pl.when(p > 0)
        def _():
            late_a_pairs(p - 1)

        @pl.when(hub & (p == 0))
        def _():
            pair(0, 16)
            pair(0, 17)

        pass_on(p, 2)

        @pl.when(p > 0)
        def _():
            late_b_pairs(p - 1)

        @pl.when(hub & (p == 0))
        def _():
            pair(0, 14)
            pair(0, 15)

        pass_on(p, 3)
        return carry

    lax.fori_loop(0, PIECES - 1, step, 0)
    last = PIECES - 1
    pass_on(last, 0)
    late_a_pairs(last - 1)
    pass_on(last, 1)
    late_b_pairs(last - 1)
    pass_on(last, 2)
    late_a_landed(last, 0)
    for at in range(EL_A):
        first_half(at, last)
    pass_on(last, 3)
    late_b_landed(last, 0)
    for at in range(EL_A, len(EL_HUB)):
        first_half(at, last)
    late_a_landed(last, 1)
    for at in range(EL_A):
        late_pair(at, last, True)
    pair(2, 0)
    late_b_landed(last, 1)
    for at in range(EL_A, len(EL_HUB)):
        late_pair(at, last, True)
    for at in range(1, 3):
        pair(2, at)

    @pl.when(hub_f == 0)
    def _():
        pair(2, 3)
        pair(2, 4)

    def give(item, to, send, device):
        return remote(best.at[item], ret.at[to], ret_send.at[send], ret_recv.at[to], device)

    def hub_gives():
        return [give(item, to, item - 1, device) for item, (to, device) in enumerate(hub_owners, 1)]

    def clus_gives():
        return [give(1, 3, 0, mate), give(5, 4, 1, dev(3, 1 - k, 0, 0)), give(6, 4, 2, dev(3, k, 0, 0)),
                give(7, 5, 3, dev(1, 1 - k, 0, 0)), give(8, 5, 4, dev(1, k, 0, 0))]

    for which, gives in ((hub, hub_gives), (hub_f == 0, clus_gives)):
        @pl.when(which)
        def _(gives=gives):
            for copy in reversed(gives()):
                copy.start()

    for s in range(2):
        arrived(early.at[0], own_send.at[s])
        arrived(meta_e.at[0], meta_send.at[s])

    @pl.when(hub)
    def _():
        for s in range(2, 6):
            arrived(early.at[0], own_send.at[s])
        for s in range(3):
            arrived(early.at[0], fwd_send.at[s])
        for s in range(2, 9):
            arrived(meta_e.at[0], meta_send.at[s])
        for s in range(7):
            arrived(best.at[0], ret_send.at[s])

    @pl.when(hub_f == 0)
    def _():
        arrived(early.at[0], own_send.at[2])
        arrived(meta_e.at[0], meta_send.at[2])
        for s in range(5):
            arrived(best.at[0], ret_send.at[s])

    result = best[0]
    for j in range(6):
        arrived(ret.at[j], ret_recv.at[j])
        result = jnp.maximum(result, ret[j])
    out[...] = result


def on_device(embeddings, labels, partner_block, own_block, live):
    dma = pltpu.SemaphoreType.DMA
    vmem = pl.BlockSpec(memory_space=pltpu.VMEM)
    best = pl.pallas_call(
        kernel,
        out_shape=jax.ShapeDtypeStruct((16, 128), jnp.float32),
        in_specs=[pl.BlockSpec(memory_space=pl.ANY)] * 5,
        out_specs=vmem,
        scratch_shapes=[
            pltpu.VMEM((5, BLOCKS, BLOCK, D), jnp.bfloat16),
            pltpu.VMEM((2, BLOCKS, BLOCK, D), jnp.bfloat16),
            pltpu.VMEM((2, BLOCKS, BLOCK, D), jnp.bfloat16),
            pltpu.VMEM((16, 128), jnp.int32),
            pltpu.VMEM((3, 1, 24), jnp.int32),
            pltpu.VMEM((5, BLOCKS + 1, 8, 128), jnp.int32),
            pltpu.VMEM((4, BLOCKS + 1, 8, 128), jnp.int32),
            pltpu.SMEM((9, 8, 128), jnp.int32),
            pltpu.VMEM((9, 16, 128), jnp.float32),
            pltpu.VMEM((len(EL_HUB), BLOCK, PIECE), jnp.float32),
            pltpu.VMEM((6, 16, 128), jnp.float32),
            dma((PIECES + 4,)), dma((9,)), dma((6,)), dma((3,)), dma((9,)), dma((7,)),
            dma((PIECES,)), dma((CHUNKS,)), dma((CHUNKS,)), dma((4, PIECES, 2)), dma((3,)), dma((9,)), dma((6,)),
        ],
        compiler_params=pltpu.CompilerParams(collective_id=0, has_side_effects=True, vmem_limit_bytes=56 << 20),
        cost_estimate=pl.CostEstimate(flops=24 * 2 * 512 * 512 * 1024, bytes_accessed=4 << 20, transcendentals=2048),
    )(embeddings, labels.reshape(16, 128), own_block, partner_block, live)
    return best.reshape(2048)


def solution(mesh):
    placed = (
        P(("clus", "grp"), None),
        P(("clus", "grp")),
        P(("clus", "grp"), None),
        P(("clus", "grp"), None),
        P(("clus", "grp"), None),
    )
    return jax.shard_map(
        on_device, mesh=mesh, in_specs=placed, out_specs=P(("clus", "grp")), check_vma=False
    )
```
